128 devices in a mesh: lat: 4 (over z), lon: 32 (over y, x, core).
Axes of the slice: x: 4, y: 4, z: 4, core: 2. Of those that a mesh axis runs over, the one named last changes fastest.
Arguments:
- conc: float32 [150, 262144], P(None, ('lat', 'lon')), may hold values from 0.2 to 2
- dest_tile: int32 [262144, 1], P(('lat', 'lon')), may hold values from 0 to 127; in each aligned block of 2048 rows (0 to 2047, 2048 to 4095, ...) at most 32 rows name the same one
- mixing_share: float32 [524288], P(('lat', 'lon')), may hold values from 0.1 to 0.6
- partner: int32 [524288], P(('lat', 'lon')), may hold values from 0 to 127
- photolysis: float32 [524288], P(('lat', 'lon')), may hold values from 0.1 to 1
- production: float32 [150], replicated, may hold values from 0.2 to 1
- loss: float32 [150], replicated, may hold values from 0.05 to 0.5
- rates: float32 [150, 150], replicated, may hold values from -0.5 to 0.5
- pattern: int32 [10, 10], replicated, may hold values 0 or 1
- precond: float32 [150, 150], replicated, may hold values from -2 to 2
Outputs:
- chem: float32 [150, 524288], P(None, ('lat', 'lon'))
The draws below stay inside these ranges and needn't reach their ends.
Inputs may be any that keep to these rules, and one draw needn't show every extreme that they name: `dest_tile`: no tile sends more than 32 parcels to one tile, and some tile sends exactly 32 to one.
All inputs are finite; a program needn't handle non-finite values.
Results may differ from the reference program's by a relative error of at most 0.0003.
Values sent between devices are 32-bit elements; how exact they have to be, the bound alone decides.
No kernel may reach another device: no remote copies, remote signals or barrier semaphores. Data moves between devices by JAX's collectives and lax.ppermute only.
A program may use at most 64 MiB of HBM per device.

```python
import math
import jax
import jax.numpy as jnp
import numpy as np
from jax import lax

NB = 10
SB = 15
SPECIES_COUNT = 150
P_DEV = 2048
MIXING_BLOCK = 128
NEWTON = 2
CAP = 32
NPARCELS = 262144
TOTAL_SLOTS = 524288
N_LAT = 4
N_LON = 32
DEVICES = 128


def draw_precond(key, part):
    key = jax.random.fold_in(key, 7)
    spread = jax.random.truncated_normal(key, -4.0, 4.0, (SPECIES_COUNT, SPECIES_COUNT), jnp.float32)
    return jnp.eye(SPECIES_COUNT, dtype=jnp.float32) + 0.3 * spread / math.sqrt(SPECIES_COUNT)


def plant(array, key, low, high):
    place = [jax.random.randint(jax.random.fold_in(key, axis), (), 0, length) for axis, length in enumerate(array.shape)]
    main_axis = array.shape.index(max(array.shape))
    neighbour = place[:main_axis] + [(place[main_axis] + 1) % array.shape[main_axis]] + place[main_axis + 1:]
    return array.at[tuple(place)].set(low).at[tuple(neighbour)].set(high)


def levels(key, shape, split, smallest, top_value):
    gain, own = 1.0, jax.random.fold_in(key, 6)
    for position, blocks in split:
        draws = jnp.exp(jax.random.uniform(jax.random.fold_in(own, position), (blocks,), jnp.float32, smallest / len(split), top_value / len(split)))
        gain = gain * jnp.repeat(draws, shape[position] // blocks).reshape([-1 if axis == position else 1 for axis in range(len(shape))])
    return gain


def routed_block(own_key, own, number, rows, amount, top, bound, slope):
    order = jax.random.permutation(own_key, amount)
    crowded, usual = shares(amount, rows * top, bound, slope, True), shares(amount, rows * top, bound, slope, False)
    places = jnp.arange(amount)

    def named(tallies, turn):
        used = int((tallies > 0).sum())
        fixed = max(1, used // 4)
        passed = fixed + (places - fixed + turn * (used - fixed)) % max(1, amount - fixed)
        return jnp.zeros((amount,), jnp.int32).at[order[jnp.where(places < fixed, places, passed)]].set(jnp.asarray(tallies, jnp.int32))

    tallies = jnp.where(number % 4 == 0, named(crowded, number // 4), named(usual, number - number // 4 - 1))
    mixed = jax.random.permutation(jax.random.fold_in(own, 3), amount)
    source_of, sink = mixed[0:amount // 2 * 2:2], mixed[1:amount // 2 * 2:2]
    margin = jnp.minimum(tallies[source_of] - 1, bound - tallies[sink]) // 2
    margin = jnp.where((source_of == order[0]) | (sink == order[0]) | (tallies[sink] == 0), 0, jnp.maximum(margin, 0))
    passed = jax.random.randint(jax.random.fold_in(own, 4), (amount // 2,), 0, 1 << 20) % (margin + 1)
    tallies = tallies.at[source_of].add(-passed).at[sink].add(passed)
    labels = jnp.searchsorted(jnp.cumsum(tallies), jnp.arange(rows * top), side="right").astype(jnp.int32)
    grid = labels.reshape(top, rows).T
    grid = grid[jax.random.permutation(jax.random.fold_in(own, 1), rows)]
    turn = jax.random.randint(jax.random.fold_in(own, 2), (rows, 1), 0, top)
    return jnp.take_along_axis(grid, (jnp.arange(top)[None, :] + turn) % top, axis=1)


def shares(amount, total, bound, lean, full):
    portions = [(1 << 20) // math.isqrt(standing ** lean) + 1 for standing in range(1, amount + 1)]
    largest = bound if full else min(bound, max(-(-total // amount), total * portions[0] // sum(portions)))
    least = 1 if total - largest >= amount - 1 else 0
    holding, rest = [largest] + [least] * (amount - 1), total - largest - least * (amount - 1)
    while rest > 0:
        movable = [i for i in range(1, amount) if holding[i] < largest] or [i for i in range(1, amount) if holding[i] < bound]
        whole, budget = sum([portions[i] for i in movable]), rest
        for i in movable:
            addition = min(bound - holding[i], max(1, budget * portions[i] // whole), rest)
            holding[i] = holding[i] + addition
            rest = rest - addition
    return np.array(holding)


def bell_draw(stream_key, dims, scale, reach, kind=jnp.bfloat16):
    array = scale * jax.random.normal(stream_key, dims, jnp.float32)
    return jnp.clip(array, min=-reach, max=reach).astype(kind)


def setup_inputs(seed: int = 0) -> dict:
    key_of = jax.random.split(jax.random.key(seed), 11)
    conc = jnp.clip(jnp.exp(math.log(2.0) - 2.3025851 * jax.random.uniform(key_of[0], (SPECIES_COUNT, NPARCELS), jnp.float32) ** levels(key_of[0], (SPECIES_COUNT, NPARCELS), ((1, 128),), -0.2, 0.2)), 0.2, 2.0)
    dest_tile_keys = jax.random.split(jax.random.fold_in(key_of[1], 1), NPARCELS // P_DEV)
    dest_tile_turns = jax.random.permutation(jax.random.fold_in(key_of[1], 3), NPARCELS // P_DEV)
    dest_tile = jax.vmap(lambda own, number: routed_block(jax.random.fold_in(key_of[1], 2), own, number, P_DEV, DEVICES, 1, CAP, 2))(dest_tile_keys, dest_tile_turns).reshape((NPARCELS, 1))
    mixing_share = jnp.clip(0.1 + 0.5 * jax.random.uniform(key_of[2], (TOTAL_SLOTS,), jnp.float32) ** levels(key_of[2], (TOTAL_SLOTS,), ((0, 128),), -0.2, 0.2), 0.1, 0.6)
    partner = plant(jax.random.randint(key_of[3], (TOTAL_SLOTS,), 0, MIXING_BLOCK), jax.random.fold_in(key_of[3], 1), 0, MIXING_BLOCK - 1).astype(jnp.int32)
    photolysis = jnp.clip(jnp.exp(math.log(1.0) - 2.3025851 * jax.random.uniform(key_of[4], (TOTAL_SLOTS,), jnp.float32) ** levels(key_of[4], (TOTAL_SLOTS,), ((0, 128),), -0.2, 0.2)), 0.1, 1.0)
    production = jnp.clip(jax.random.uniform(key_of[5], (SPECIES_COUNT,), jnp.float32, 0.2, 1.0), 0.2, 1.0)
    loss = jnp.clip(jnp.exp(jax.random.uniform(key_of[6], (SPECIES_COUNT,), jnp.float32, math.log(0.05), math.log(0.5))), 0.05, 0.5)
    rates = bell_draw(key_of[7], (SPECIES_COUNT, SPECIES_COUNT), SPECIES_COUNT ** -0.5, 0.5, jnp.float32)
    pattern = plant((jax.random.randint(key_of[8], (NB, NB), 0, 2) < 1).astype(jnp.int32), jax.random.fold_in(key_of[8], 1), 0, 1)
    precond = draw_precond(jax.random.fold_in(key_of[10], 71), 0)
    return {"conc": conc, "dest_tile": dest_tile, "mixing_share": mixing_share, "partner": partner, "photolysis": photolysis, "production": production, "loss": loss, "rates": rates, "pattern": pattern, "precond": precond}


time_step = 0.5


def block_mask(pattern):
    return jnp.kron(pattern.astype(jnp.float32), jnp.ones((SB, SB), jnp.float32))


def chemistry(initial, photo_rate, present_mask, coupled, production, loss, precond):
    current = initial
    for iteration in range(NEWTON):
        tendency = jnp.dot(coupled, current, precision=lax.Precision.HIGHEST, preferred_element_type=jnp.float32)
        tendency = tendency + production[:, None] * photo_rate[None, :] - loss[:, None] * current * current
        misfit = current - initial - time_step * tendency
        first_pass = jnp.dot(precond, misfit, precision=lax.Precision.HIGHEST, preferred_element_type=jnp.float32)
        second_pass = jnp.dot(precond, 2.0 * time_step * loss[:, None] * current * first_pass, precision=lax.Precision.HIGHEST, preferred_element_type=jnp.float32)
        current = current - (first_pass - second_pass)
    return current * present_mask[None, :]


def ranks_within(targets):
    columns = jnp.arange(DEVICES, dtype=jnp.int32)
    onehot = (targets[:, None] == columns[None, :]).astype(jnp.int32)
    before = jnp.cumsum(onehot, axis=0) - onehot
    return jnp.sum(before * onehot, axis=1).astype(jnp.int32)


def reference(conc, dest_tile, mixing_share, partner, photolysis, production, loss, rates, pattern, precond):
    tile_slots = DEVICES * CAP
    targets = dest_tile[:, 0].astype(jnp.int32).reshape(DEVICES, P_DEV)
    ranking = lax.map(ranks_within, targets)
    sources = jnp.arange(DEVICES, dtype=jnp.int32)[:, None]
    arrival_slot = (targets * tile_slots + sources * CAP + ranking).reshape(-1)
    placed_parcels = jnp.zeros((SPECIES_COUNT, TOTAL_SLOTS), jnp.float32).at[:, arrival_slot].set(conc)
    present_mask = jnp.zeros((TOTAL_SLOTS,), jnp.float32).at[arrival_slot].set(1.0)
    gridded = placed_parcels.reshape(SPECIES_COUNT, N_LAT, N_LON, tile_slots)
    eastern = jnp.roll(gridded, -1, axis=2)
    present_grid = present_mask.reshape(N_LAT, N_LON, tile_slots)
    present_east = jnp.roll(present_grid, -1, axis=1)
    local_pos = jnp.arange(tile_slots, dtype=jnp.int32)
    partner_slot = ((local_pos // MIXING_BLOCK) * MIXING_BLOCK)[None, None, :] + partner.astype(jnp.int32).reshape(N_LAT, N_LON, tile_slots)
    partner_conc = jnp.take_along_axis(eastern, partner_slot[None], axis=3)
    partner_alive = jnp.take_along_axis(present_east, partner_slot, axis=2)
    weight_mix = mixing_share.reshape(N_LAT, N_LON, tile_slots) * present_grid * partner_alive
    mixed = gridded + weight_mix[None] * (partner_conc - gridded)
    coupled = rates * block_mask(pattern)
    per_tile = jnp.moveaxis(mixed.reshape(SPECIES_COUNT, DEVICES, tile_slots), 1, 0)
    photo_tiles = photolysis.reshape(DEVICES, tile_slots)
    present_tiles = present_mask.reshape(DEVICES, tile_slots)
    final_output = lax.map(lambda members: chemistry(members[0], members[1], members[2], coupled, production, loss, precond), (per_tile, photo_tiles, present_tiles))
    return jnp.moveaxis(final_output, 0, 1).reshape(SPECIES_COUNT, TOTAL_SLOTS)
```

```python
import functools

import jax
import jax.numpy as jnp
from jax import lax
from jax.experimental import pallas as pl
from jax.experimental.pallas import tpu as pltpu
from jax.sharding import PartitionSpec as P

SB = 15
NEWTON = 2
time_step = 0.5

LANES = 128
CAP = 32
QUARTER = 40
ROWS = 4 * QUARTER
TILES = QUARTER // 8


def regroup(first, second, third, fourth, lane):
    low_half = lane < 64
    low_quarter = (lane % 64) < 32
    t0 = jnp.where(low_half, first, pltpu.roll(third, 64, 1))
    t2 = jnp.where(low_half, pltpu.roll(first, 64, 1), third)
    t1 = jnp.where(low_half, second, pltpu.roll(fourth, 64, 1))
    t3 = jnp.where(low_half, pltpu.roll(second, 64, 1), fourth)
    return (
        jnp.where(low_quarter, t0, pltpu.roll(t1, 32, 1)),
        jnp.where(low_quarter, pltpu.roll(t0, 96, 1), t1),
        jnp.where(low_quarter, t2, pltpu.roll(t3, 32, 1)),
        jnp.where(low_quarter, pltpu.roll(t2, 96, 1), t3),
    )


def slot_table(targets_ref):
    blocks = targets_ref.shape[0]
    row = lax.broadcasted_iota(jnp.int32, (LANES, LANES), 0)
    column = lax.broadcasted_iota(jnp.int32, (LANES, LANES), 1)
    earlier = (row < column).astype(jnp.float32).astype(jnp.bfloat16)
    ones = jnp.ones((LANES, LANES), jnp.bfloat16)
    counted = jnp.zeros((LANES, LANES), jnp.float32)
    table = jnp.zeros((3 * CAP, LANES), jnp.float32)
    group = lax.broadcasted_iota(jnp.int32, (CAP, LANES), 0)
    place = lax.broadcasted_iota(jnp.int32, (CAP, LANES), 1).astype(jnp.float32)
    for block in range(blocks):
        targets = targets_ref[block : block + 1, :]
        onehot = (row == targets).astype(jnp.float32)
        packed = onehot.astype(jnp.bfloat16)
        before = jnp.dot(packed, earlier, preferred_element_type=jnp.float32)
        ranking = jnp.sum(onehot * (before + counted), axis=0, keepdims=True)
        counted = counted + jnp.dot(packed, ones, preferred_element_type=jnp.float32)
        slot = targets * CAP + ranking.astype(jnp.int32)
        here = (row == slot % LANES).astype(jnp.float32).astype(jnp.bfloat16)
        mine = (group == slot // LANES).astype(jnp.float32)
        left = jnp.concatenate([mine, mine * float(block), mine * place], axis=0)
        table = table + lax.dot_general(
            left.astype(jnp.bfloat16),
            here,
            (((1,), (1,)), ((), ())),
            preferred_element_type=jnp.float32,
        )
    return table


def pack_kernel(conc_ref, targets_ref, out_ref, padded, table_ref):
    species, parcels = conc_ref.shape
    blocks = parcels // LANES
    whole = species // 8 * 8
    padded[whole:ROWS, :] = jnp.zeros((ROWS - whole, parcels), jnp.float32)
    padded[0:species, :] = conc_ref[...]
    table_ref[...] = slot_table(targets_ref).astype(jnp.int32)
    lane = lax.broadcasted_iota(jnp.int32, (8, LANES), 1)

    def step(group, carry):
        filled = jnp.broadcast_to(table_ref[pl.ds(group, 1), :], (8, LANES))
        block = jnp.broadcast_to(table_ref[pl.ds(CAP + group, 1), :], (8, LANES))
        place = jnp.broadcast_to(table_ref[pl.ds(2 * CAP + group, 1), :], (8, LANES))
        block = jnp.where(filled > 0, block, -1)
        masks = [block == b for b in range(blocks)]
        for k in range(TILES):
            parts = []
            for j in range(4):
                base = QUARTER * j + 8 * k
                if base >= species:
                    parts.append(jnp.zeros((8, LANES), jnp.float32))
                    continue
                value = jnp.zeros((8, LANES), jnp.float32)
                for b in range(blocks):
                    source = padded[base : base + 8, b * LANES : (b + 1) * LANES]
                    value = jnp.where(
                        masks[b], jnp.take_along_axis(source, place, axis=1), value
                    )
                parts.append(value)
            for d, chunk in enumerate(regroup(*parts, lane)):
                out_ref[group * 4 + d, 8 * k : 8 * k + 8, :] = chunk
        return carry

    lax.fori_loop(0, CAP, step, 0)


def pack(conc, targets):
    devices = 128
    species, parcels = conc.shape
    return pl.pallas_call(
        pack_kernel,
        out_shape=jax.ShapeDtypeStruct((devices, QUARTER, LANES), jnp.float32),
        in_specs=[pl.BlockSpec(memory_space=pltpu.VMEM)] * 2,
        out_specs=pl.BlockSpec(memory_space=pltpu.VMEM),
        scratch_shapes=[
            pltpu.VMEM((ROWS, parcels), jnp.float32),
            pltpu.VMEM((3 * CAP, LANES), jnp.int32),
        ],
        compiler_params=pltpu.CompilerParams(vmem_limit_bytes=32 * 1024 * 1024),
        name="pack",
    )(conc, targets)


def product(weights, value):
    high = value.astype(jnp.bfloat16)
    low = (value - high.astype(jnp.float32)).astype(jnp.bfloat16)
    return jnp.dot(
        weights,
        jnp.concatenate([high, low, high], axis=0),
        preferred_element_type=jnp.float32,
    )


def react_kernel(
    own_ref, east_ref, share_ref, partner_ref, photo_ref, coupled_ref, precond_ref, production_ref, loss_ref, *rest
):
    out_ref, mixed_ref, present_ref = rest[-3:]
    blocks = own_ref.shape[0] // 4
    species = out_ref.shape[0]
    lane = lax.broadcasted_iota(jnp.int32, (8, LANES), 1)
    step = pl.program_id(0)
    for m in range(blocks):
        span = slice(m * LANES, (m + 1) * LANES)
        index = jnp.broadcast_to(partner_ref[pl.ds(m, 1), :], (8, LANES))
        weight = None
        for k in range(TILES):
            rows = slice(8 * k, 8 * k + 8)
            own = regroup(*[own_ref[4 * m + s, rows, :] for s in range(4)], lane)
            east = regroup(*[east_ref[4 * m + s, rows, :] for s in range(4)], lane)
            for j in range(4):
                base = QUARTER * j + 8 * k
                chosen = jnp.take_along_axis(east[j], index, axis=1)
                if weight is None:
                    present = (own[0][0:1] > 0.0).astype(jnp.float32)
                    alive = (chosen[0:1] > 0.0).astype(jnp.float32)
                    weight = share_ref[pl.ds(m, 1), :] * present * alive
                    present_ref[:, span] = present
                mixed_ref[base : base + 8, span] = own[j] + weight * (chosen - own[j])
    width = blocks * LANES
    photo = jnp.concatenate([photo_ref[pl.ds(m, 1), :] for m in range(blocks)], axis=1)
    initial = mixed_ref[...]
    loss = jnp.broadcast_to(loss_ref[:, 0:1], (ROWS, width))
    source = jnp.broadcast_to(production_ref[:, 0:1], (ROWS, width)) * photo
    current = initial
    for _ in range(NEWTON):
        tendency = product(coupled_ref[...], current) + source - loss * current * current
        misfit = current - initial - time_step * tendency
        first_pass = product(precond_ref[...], misfit)
        second_pass = product(precond_ref[...], 2.0 * time_step * loss * current * first_pass)
        current = current - (first_pass - second_pass)
    result = current * present_ref[...]
    out_ref[...] = result[:species]


def react(part, parts, species, own, east, share, partner, photo, weights, so_far):
    sources = own.shape[0]
    blocks = 8
    steps = sources // (4 * blocks) // parts
    width = blocks * LANES
    first = part * steps

    def at_own(i):
        return (first + i, 0, 0)

    def at_east(i):
        return (i, 0, 0)

    def at_row(i):
        return (first + i, 0)

    def once(i):
        return (0, 0)

    in_specs = [
        pl.BlockSpec((4 * blocks, QUARTER, LANES), at_own),
        pl.BlockSpec((4 * blocks, QUARTER, LANES), at_east),
        pl.BlockSpec((blocks, LANES), at_row),
        pl.BlockSpec((blocks, LANES), at_row),
        pl.BlockSpec((blocks, LANES), at_row),
        pl.BlockSpec((ROWS, 3 * ROWS), once),
        pl.BlockSpec((ROWS, 3 * ROWS), once),
        pl.BlockSpec((ROWS, LANES), once),
        pl.BlockSpec((ROWS, LANES), once),
    ]
    operands = [own, east, share, partner, photo, *weights]
    aliases = {}
    if so_far is not None:
        in_specs.append(pl.BlockSpec(memory_space=pl.ANY))
        operands.append(so_far)
        aliases = {len(operands) - 1: 0}
    columns = steps * width
    return pl.pallas_call(
        react_kernel,
        grid=(steps,),
        out_shape=jax.ShapeDtypeStruct((species, sources * CAP), jnp.float32),
        in_specs=in_specs,
        out_specs=pl.BlockSpec((species, width), lambda i: (0, first + i)),
        scratch_shapes=[
            pltpu.VMEM((ROWS, width), jnp.float32),
            pltpu.VMEM((1, width), jnp.float32),
        ],
        input_output_aliases=aliases,
        compiler_params=pltpu.CompilerParams(vmem_limit_bytes=48 * 1024 * 1024),
        cost_estimate=pl.CostEstimate(
            flops=6 * 2 * 256 * 512 * columns, bytes_accessed=12 * ROWS * columns, transcendentals=0
        ),
        name="react",
    )(*operands)


def split(matrix):
    size = matrix.shape[0]
    padded = jnp.pad(matrix, ((0, ROWS - size), (0, ROWS - size)))
    high = lax.reduce_precision(padded, 8, 7)
    low = padded - high
    return jnp.concatenate([high, high, low], axis=1).astype(jnp.bfloat16)


def column(vector):
    return jnp.broadcast_to(jnp.pad(vector, (0, ROWS - vector.shape[0]))[:, None], (ROWS, LANES))


PARTS = 2


def shards(
    conc, dest_tile, mixing_share, partner, photolysis, production, loss, rates, pattern, precond
):
    species, parcels = conc.shape
    packed = pack(conc, dest_tile.reshape(parcels // LANES, LANES))
    arrived = lax.all_to_all(packed, ("lat", "lon"), split_axis=0, concat_axis=0, tiled=True)
    lon_count = lax.axis_size("lon")
    west = [(source, (source - 1) % lon_count) for source in range(lon_count)]
    length = arrived.shape[0] // PARTS
    eastern = [
        lax.ppermute(arrived[part * length : (part + 1) * length], "lon", west) for part in range(PARTS)
    ]
    coupled = rates * jnp.kron(pattern.astype(jnp.float32), jnp.ones((SB, SB), jnp.float32))
    weights = (split(coupled), split(precond), column(production), column(loss))
    rows = mixing_share.shape[0] // LANES
    share, index, photo = (a.reshape(rows, LANES) for a in (mixing_share, partner, photolysis))
    result = None
    for part in range(PARTS):
        result = react(
            part, PARTS, species, arrived, eastern[part], share, index, photo, weights, result
        )
    return result


def solution(mesh):
    placed = (
        P(None, ("lat", "lon")),
        P(("lat", "lon"), None),
        P(("lat", "lon")),
        P(("lat", "lon")),
        P(("lat", "lon")),
        P(),
        P(),
        P(),
        P(),
        P(),
    )
    return jax.shard_map(
        shards, mesh=mesh, in_specs=placed, out_specs=P(None, ("lat", "lon")), check_vma=False
    )
```

```python
import jax
import jax.numpy as jnp
from jax import lax
from jax.experimental import pallas as pl
from jax.experimental.pallas import tpu as pltpu
from jax.sharding import Mesh
from jax.sharding import PartitionSpec as P

SB = 15
NEWTON = 2
time_step = 0.5

LANES = 128
CAP = 32
QUARTER = 40
ROWS = 4 * QUARTER
TILES = QUARTER // 8
GROUP = 256
TOGETHER = 4


def regroup(first, second, third, fourth, lane):
    low_half = lane < 64
    low_quarter = (lane % 64) < 32
    t0 = jnp.where(low_half, first, pltpu.roll(third, 64, 1))
    t2 = jnp.where(low_half, pltpu.roll(first, 64, 1), third)
    t1 = jnp.where(low_half, second, pltpu.roll(fourth, 64, 1))
    t3 = jnp.where(low_half, pltpu.roll(second, 64, 1), fourth)
    return (
        jnp.where(low_quarter, t0, pltpu.roll(t1, 32, 1)),
        jnp.where(low_quarter, pltpu.roll(t0, 96, 1), t1),
        jnp.where(low_quarter, t2, pltpu.roll(t3, 32, 1)),
        jnp.where(low_quarter, pltpu.roll(t2, 96, 1), t3),
    )


def pack_kernel(core_ref, conc_ref, targets_ref, out_ref, parts_ref, place_ref, group_ref, sums_ref):
    species, parcels = conc_ref.shape
    row = lax.broadcasted_iota(jnp.int32, (LANES, LANES), 0)
    column = lax.broadcasted_iota(jnp.int32, (LANES, LANES), 1)
    earlier = (row < column).astype(jnp.float32).astype(jnp.bfloat16)
    sums_of = jnp.concatenate([earlier, jnp.ones((LANES, LANES), jnp.bfloat16)], axis=1)
    counted = jnp.zeros((LANES, LANES), jnp.float32)
    for block in range(parcels // LANES):
        span = slice(block * LANES, (block + 1) * LANES)
        targets = targets_ref[block : block + 1, :]
        onehot = (row == targets).astype(jnp.float32)
        sums = jnp.dot(onehot.astype(jnp.bfloat16), sums_of, preferred_element_type=jnp.float32)
        ranking = jnp.sum(onehot * (sums[:, :LANES] + counted), axis=0, keepdims=True)
        counted = counted + sums[:, LANES:]
        slot = targets * CAP + ranking.astype(jnp.int32)
        group_ref[:, span] = jnp.broadcast_to(slot // GROUP, (16, LANES))
        place = jnp.broadcast_to((slot % GROUP).astype(jnp.float32), (LANES, LANES))
        place = jnp.transpose(place).astype(jnp.int32)
        for half in range(GROUP // LANES):
            here = (place == column + half * LANES).astype(jnp.float32)
            place_ref[span, half * LANES : (half + 1) * LANES] = here.astype(jnp.bfloat16)
    conc = conc_ref[...]
    low = conc - conc.astype(jnp.bfloat16).astype(jnp.float32)
    filler = jnp.zeros((ROWS - species, parcels), jnp.float32)
    parts_ref[0:ROWS, :] = jnp.concatenate([conc, filler], axis=0).astype(jnp.bfloat16)
    parts_ref[ROWS:, :] = jnp.concatenate([low, filler], axis=0).astype(jnp.bfloat16)
    lane = lax.broadcasted_iota(jnp.int32, (8, LANES), 1)
    core = core_ref[0]
    around = out_ref.shape[0] // 4

    def step(i, carry):
        chosen = []
        for t in range(TOGETHER):
            mine = (group_ref[...] == i * TOGETHER + t).astype(jnp.float32).astype(jnp.bfloat16)
            chosen.append(parts_ref[...] * jnp.concatenate([mine] * (2 * ROWS // 16), axis=0))
        moved = jnp.dot(
            jnp.concatenate(chosen, axis=0), place_ref[...], preferred_element_type=jnp.float32
        )
        for t in range(TOGETHER):
            base = 2 * t * ROWS
            sums_ref[...] = moved[base : base + ROWS] + moved[base + ROWS : base + 2 * ROWS]
            for half in range(GROUP // LANES):
                span = slice(half * LANES, (half + 1) * LANES)
                quad = (i * TOGETHER + t) * (GROUP // LANES) + half
                for k in range(TILES):
                    rows = slice(8 * k, 8 * k + 8)
                    quarters = [sums_ref[QUARTER * j + 8 * k : QUARTER * j + 8 * k + 8, span] for j in range(4)]
                    for d, chunk in enumerate(regroup(*quarters, lane)):
                        chip = quad * 2 + d // 2
                        odd = d % 2
                        out_ref[chip, jnp.where(core == 0, odd, 2 - odd), rows, :] = chunk
                        if not odd:
                            west = chip // around * around + (chip + around - 1) % around
                            out_ref[west, jnp.where(core == 0, 2, 0), rows, :] = chunk
        return carry

    lax.fori_loop(0, 16 // TOGETHER, step, 0)


def pack(core, conc, targets, chips):
    parcels = conc.shape[1]
    in_vmem = pl.BlockSpec(memory_space=pltpu.VMEM)
    return pl.pallas_call(
        pack_kernel,
        out_shape=jax.ShapeDtypeStruct((chips, 3, QUARTER, LANES), jnp.float32),
        in_specs=[pl.BlockSpec(memory_space=pltpu.SMEM), in_vmem, in_vmem],
        out_specs=in_vmem,
        scratch_shapes=[
            pltpu.VMEM((2 * ROWS, parcels), jnp.bfloat16),
            pltpu.VMEM((parcels, GROUP), jnp.bfloat16),
            pltpu.VMEM((16, parcels), jnp.int32),
            pltpu.VMEM((ROWS, GROUP), jnp.float32),
        ],
        compiler_params=pltpu.CompilerParams(vmem_limit_bytes=40 * 1024 * 1024),
        name="pack",
    )(core, conc, targets)


def product(weights, value):
    high = value.astype(jnp.bfloat16)
    low = (value - high.astype(jnp.float32)).astype(jnp.bfloat16)
    return jnp.dot(
        weights,
        jnp.concatenate([high, low, high], axis=0),
        preferred_element_type=jnp.float32,
    )


def react_kernel(
    core_ref, mine_ref, other_ref, share_ref, partner_ref, photo_ref, coupled_ref, precond_ref, production_ref, loss_ref, *rest
):
    out_ref, mixed_ref, present_ref = rest[-3:]
    blocks = mine_ref.shape[0] // 2
    core = core_ref[0]
    species = out_ref.shape[0]
    lane = lax.broadcasted_iota(jnp.int32, (8, LANES), 1)

    def sources(m, rows, at_mine, at_other):
        parts = []
        for chip in (2 * m, 2 * m + 1):
            mine = mine_ref[chip, at_mine, rows, :]
            other = other_ref[chip, at_other, rows, :]
            parts += [jnp.where(core == 0, mine, other), jnp.where(core == 0, other, mine)]
        return parts

    for m in range(blocks):
        span = slice(m * LANES, (m + 1) * LANES)
        index = jnp.broadcast_to(partner_ref[pl.ds(m, 1), :], (8, LANES))
        weight = None
        for k in range(TILES):
            rows = slice(8 * k, 8 * k + 8)
            own = regroup(*sources(m, rows, core, 1 - core), lane)
            east = regroup(*sources(m, rows, 1 - core, core), lane)
            for j in range(4):
                base = QUARTER * j + 8 * k
                chosen = jnp.take_along_axis(east[j], index, axis=1)
                if weight is None:
                    present = (own[0][0:1] > 0.0).astype(jnp.float32)
                    alive = (chosen[0:1] > 0.0).astype(jnp.float32)
                    weight = share_ref[pl.ds(m, 1), :] * present * alive
                    present_ref[:, span] = present
                mixed_ref[base : base + 8, span] = own[j] + weight * (chosen - own[j])
    width = blocks * LANES
    photo = jnp.concatenate([photo_ref[pl.ds(m, 1), :] for m in range(blocks)], axis=1)
    initial = mixed_ref[...]
    loss = jnp.broadcast_to(loss_ref[:, 0:1], (ROWS, width))
    source = jnp.broadcast_to(production_ref[:, 0:1], (ROWS, width)) * photo
    current = initial
    for _ in range(NEWTON):
        tendency = product(coupled_ref[...], current) + source - loss * current * current
        misfit = current - initial - time_step * tendency
        first_pass = product(precond_ref[...], misfit)
        second_pass = product(precond_ref[...], 2.0 * time_step * loss * current * first_pass)
        current = current - (first_pass - second_pass)
    result = current * present_ref[...]
    out_ref[...] = result[:species]


def react(part, parts, species, core, mine, other, share, partner, photo, weights, so_far):
    chips = mine.shape[0]
    blocks = 8
    steps = chips // (2 * blocks) // parts
    width = blocks * LANES
    first = part * steps

    def at_row(i):
        return (first + i, 0)

    def once(i):
        return (0, 0)

    in_specs = [
        pl.BlockSpec(memory_space=pltpu.SMEM),
        pl.BlockSpec((2 * blocks, 2, QUARTER, LANES), lambda i: (first + i, 0, 0, 0)),
        pl.BlockSpec((2 * blocks, 2, QUARTER, LANES), lambda i: (i, 0, 0, 0)),
        pl.BlockSpec((blocks, LANES), at_row),
        pl.BlockSpec((blocks, LANES), at_row),
        pl.BlockSpec((blocks, LANES), at_row),
        pl.BlockSpec((ROWS, 3 * ROWS), once),
        pl.BlockSpec((ROWS, 3 * ROWS), once),
        pl.BlockSpec((ROWS, LANES), once),
        pl.BlockSpec((ROWS, LANES), once),
    ]
    operands = [core, mine, other, share, partner, photo, *weights]
    aliases = {}
    if so_far is not None:
        in_specs.append(pl.BlockSpec(memory_space=pl.ANY))
        operands.append(so_far)
        aliases = {len(operands) - 1: 0}
    columns = steps * width
    return pl.pallas_call(
        react_kernel,
        grid=(steps,),
        out_shape=jax.ShapeDtypeStruct((species, chips * 2 * CAP), jnp.float32),
        in_specs=in_specs,
        out_specs=pl.BlockSpec((species, width), lambda i: (0, first + i)),
        scratch_shapes=[
            pltpu.VMEM((ROWS, width), jnp.float32),
            pltpu.VMEM((1, width), jnp.float32),
        ],
        input_output_aliases=aliases,
        compiler_params=pltpu.CompilerParams(vmem_limit_bytes=48 * 1024 * 1024),
        cost_estimate=pl.CostEstimate(
            flops=6 * 2 * 256 * 512 * columns, bytes_accessed=12 * ROWS * columns, transcendentals=0
        ),
        name="react",
    )(*operands)


def split(matrix):
    size = matrix.shape[0]
    padded = jnp.pad(matrix, ((0, ROWS - size), (0, ROWS - size)))
    high = lax.reduce_precision(padded, 8, 7)
    low = padded - high
    return jnp.concatenate([high, high, low], axis=1).astype(jnp.bfloat16)


def column(vector):
    return jnp.broadcast_to(jnp.pad(vector, (0, ROWS - vector.shape[0]))[:, None], (ROWS, LANES))


PARTS = 2


def shards(
    conc, dest_tile, mixing_share, partner, photolysis, production, loss, rates, pattern, precond
):
    species, parcels = conc.shape
    chips = lax.axis_size("lat") * lax.axis_size("chip")
    core = lax.axis_index("core").astype(jnp.int32)[None]
    packed = pack(core, conc, dest_tile.reshape(parcels // LANES, LANES), chips)
    arrived = lax.all_to_all(packed, ("lat", "chip"), split_axis=0, concat_axis=0, tiled=True)
    length = chips // PARTS
    others = [
        lax.ppermute(arrived[part * length : (part + 1) * length, 1:], "core", ((0, 1), (1, 0)))
        for part in range(PARTS)
    ]
    coupled = rates * jnp.kron(pattern.astype(jnp.float32), jnp.ones((SB, SB), jnp.float32))
    weights = (split(coupled), split(precond), column(production), column(loss))
    rows = mixing_share.shape[0] // LANES
    share, index, photo = (a.reshape(rows, LANES) for a in (mixing_share, partner, photolysis))
    result = None
    for part in range(PARTS):
        result = react(
            part, PARTS, species, core, arrived, others[part], share, index, photo, weights, result
        )
    return result


def solution(mesh):
    lat_count, lon_count = mesh.devices.shape
    by_core = Mesh(mesh.devices.reshape(lat_count, lon_count // 2, 2), ("lat", "chip", "core"))
    tiles = ("lat", "chip", "core")
    placed = (P(None, tiles), P(tiles, None), P(tiles), P(tiles), P(tiles), P(), P(), P(), P(), P())
    return jax.shard_map(
        shards, mesh=by_core, in_specs=placed, out_specs=P(None, tiles), check_vma=False
    )
```

```python
import jax
import jax.numpy as jnp
from jax import lax
from jax.experimental import pallas as pl
from jax.experimental.pallas import tpu as pltpu
from jax.sharding import Mesh
from jax.sharding import PartitionSpec as P

SB = 15
NEWTON = 2
time_step = 0.5

LANES = 128
CAP = 32
QUARTER = 20
HALF = 4 * QUARTER
ROWS = 2 * HALF
CHUNK = 3 * QUARTER
GROUP = 256
TOGETHER = 4
PARTS = 2


def regroup(parts):
    first, second, third, fourth = parts
    lane = lax.broadcasted_iota(jnp.int32, first.shape, 1)
    low_half = (lane & 64) == 0
    low_quarter = (lane & 32) == 0
    other_quarter = lane ^ 32

    def halves(a, b):
        moved = pltpu.roll(jnp.where(low_half, b, a), 64, 1)
        return jnp.where(low_half, a, moved), jnp.where(low_half, moved, b)

    def quarters(a, b):
        moved = jnp.take_along_axis(jnp.where(low_quarter, b, a), other_quarter, axis=1)
        return jnp.where(low_quarter, a, moved), jnp.where(low_quarter, moved, b)

    t0, t2 = halves(first, third)
    t1, t3 = halves(second, fourth)
    return (*quarters(t0, t1), *quarters(t2, t3))


def pack_kernel(conc_ref, targets_ref, out_ref, parts_ref, place_ref, group_ref, sums_ref):
    species, parcels = conc_ref.shape
    row = lax.broadcasted_iota(jnp.int32, (LANES, LANES), 0)
    column = lax.broadcasted_iota(jnp.int32, (LANES, LANES), 1)
    earlier = (row < column).astype(jnp.float32).astype(jnp.bfloat16)
    sums_of = jnp.concatenate([earlier, jnp.ones((LANES, LANES), jnp.bfloat16)], axis=1)
    counted = jnp.zeros((LANES, LANES), jnp.float32)
    for block in range(parcels // LANES):
        span = slice(block * LANES, (block + 1) * LANES)
        targets = targets_ref[block : block + 1, :]
        onehot = (row == targets).astype(jnp.float32)
        sums = jnp.dot(onehot.astype(jnp.bfloat16), sums_of, preferred_element_type=jnp.float32)
        ranking = jnp.sum(onehot * (sums[:, :LANES] + counted), axis=0, keepdims=True)
        counted = counted + sums[:, LANES:]
        slot = targets * CAP + ranking.astype(jnp.int32)
        group_ref[:, span] = jnp.broadcast_to(slot // GROUP, (16, LANES))
        place = jnp.broadcast_to((slot % GROUP).astype(jnp.float32), (LANES, LANES))
        place = jnp.transpose(place).astype(jnp.int32)
        for side in range(GROUP // LANES):
            here = (place == column + side * LANES).astype(jnp.float32)
            place_ref[span, side * LANES : (side + 1) * LANES] = here.astype(jnp.bfloat16)
    conc = conc_ref[...]
    low = conc - conc.astype(jnp.bfloat16).astype(jnp.float32)
    filler = jnp.zeros((ROWS - species, parcels), jnp.float32)
    parts_ref[0:ROWS, :] = jnp.concatenate([conc, filler], axis=0).astype(jnp.bfloat16)
    parts_ref[ROWS:, :] = jnp.concatenate([low, filler], axis=0).astype(jnp.bfloat16)
    around = 16

    def step(i, carry):
        chosen = []
        for t in range(TOGETHER):
            mine = (group_ref[...] == i * TOGETHER + t).astype(jnp.float32).astype(jnp.bfloat16)
            chosen.append(parts_ref[...] * jnp.concatenate([mine] * (2 * ROWS // 16), axis=0))
        moved = jnp.dot(
            jnp.concatenate(chosen, axis=0), place_ref[...], preferred_element_type=jnp.float32
        )
        for t in range(TOGETHER):
            base = 2 * t * ROWS
            sums = moved[base : base + ROWS] + moved[base + ROWS : base + 2 * ROWS]
            for side in range(GROUP // LANES):
                sums_ref[t, side] = sums[:, side * LANES : (side + 1) * LANES]
        for t in range(TOGETHER):
            for side in range(GROUP // LANES):
                quad = (i * TOGETHER + t) * (GROUP // LANES) + side
                for half in range(2):
                    quarters = [
                        sums_ref[t, side, half * HALF + QUARTER * j : half * HALF + QUARTER * (j + 1), :]
                        for j in range(4)
                    ]
                    for d, chunk in enumerate(regroup(quarters)):
                        chip = quad * 2 + d // 2
                        to = (chip * 2 + half) * CHUNK + (d % 2) * QUARTER
                        out_ref[pl.ds(to, QUARTER), :] = chunk
                        if d % 2 == 0:
                            west = chip // around * around + (chip + around - 1) % around
                            to = (west * 2 + half) * CHUNK + 2 * QUARTER
                            out_ref[pl.ds(to, QUARTER), :] = chunk
        return carry

    lax.fori_loop(0, 16 // TOGETHER, step, 0)


IN_VMEM = pl.BlockSpec(memory_space=pltpu.VMEM)
IN_SMEM = pl.BlockSpec(memory_space=pltpu.SMEM)


def pack(conc, targets, devices):
    parcels = conc.shape[1]
    return pl.pallas_call(
        pack_kernel,
        out_shape=jax.ShapeDtypeStruct((devices * CHUNK, LANES), jnp.float32),
        in_specs=[IN_VMEM, IN_VMEM],
        out_specs=IN_VMEM,
        scratch_shapes=[
            pltpu.VMEM((2 * ROWS, parcels), jnp.bfloat16),
            pltpu.VMEM((parcels, GROUP), jnp.bfloat16),
            pltpu.VMEM((16, parcels), jnp.int32),
            pltpu.VMEM((TOGETHER, GROUP // LANES, ROWS, LANES), jnp.float32),
        ],
        compiler_params=pltpu.CompilerParams(vmem_limit_bytes=40 * 1024 * 1024),
        name="pack",
    )(conc, targets)


def mix_kernel(first, core_ref, arrived_ref, share_ref, partner_ref, keep_ref, give_ref):
    blocks = keep_ref.shape[0]
    core = core_ref[0]

    def body(m, carry):
        tiles = []
        for tile in range(3):
            parts = []
            for s in range(4):
                start = ((first + m) * 4 + s) * CHUNK + tile * QUARTER
                parts.append(arrived_ref[pl.ds(start, QUARTER), :])
            tiles.append(regroup(parts))
        mixed = []
        for tile in range(2):
            own, east = tiles[tile], tiles[tile + 1]
            place = tile * 32 + first + m
            index = jnp.broadcast_to(partner_ref[pl.ds(place, 1), :], (QUARTER, LANES))
            chosen = [jnp.take_along_axis(e, index, axis=1) for e in east]
            present = (own[0][0:1] > 0.0).astype(jnp.float32)
            alive = (chosen[0][0:1] > 0.0).astype(jnp.float32)
            weight = share_ref[pl.ds(place, 1), :] * present * alive
            weight = jnp.broadcast_to(weight, (QUARTER, LANES))
            mixed.append([o + weight * (c - o) for o, c in zip(own, chosen)])
        for j in range(4):
            rows = slice(QUARTER * j, QUARTER * (j + 1))
            keep_ref[m, rows, :] = jnp.where(core == 0, mixed[0][j], mixed[1][j])
            give_ref[m, rows, :] = jnp.where(core == 0, mixed[1][j], mixed[0][j])
        return carry

    lax.fori_loop(0, blocks, body, 0, unroll=2)


def mix(part, core, arrived, share, partner):
    blocks = arrived.shape[0] // (4 * CHUNK) // PARTS
    shape = jax.ShapeDtypeStruct((blocks, HALF, LANES), jnp.float32)

    def kernel(*refs):
        mix_kernel(part * blocks, *refs)

    return pl.pallas_call(
        kernel,
        out_shape=(shape, shape),
        in_specs=[IN_SMEM, IN_VMEM, IN_VMEM, IN_VMEM],
        out_specs=(IN_VMEM, IN_VMEM),
        compiler_params=pltpu.CompilerParams(vmem_limit_bytes=16 * 1024 * 1024),
        cost_estimate=pl.CostEstimate(flops=0, bytes_accessed=8 * 1024 * 1024, transcendentals=0),
        name="mix",
    )(core, arrived, share, partner)


def product(weights, value):
    high = value.astype(jnp.bfloat16)
    low = (value - high.astype(jnp.float32)).astype(jnp.bfloat16)
    return jnp.dot(
        weights,
        jnp.concatenate([high, low, high], axis=0),
        preferred_element_type=jnp.float32,
    )


def react_kernel(
    first, core_ref, mine_ref, other_ref, photo_ref, coupled_ref, precond_ref, production_ref, loss_ref, *rest
):
    out_ref, result_ref, sems = rest[-3:]
    blocks = mine_ref.shape[0]
    steps = result_ref.shape[0]
    each = blocks // steps
    width = each * LANES
    species = out_ref.shape[0]
    core = core_ref[0]
    copies = []
    for step in range(steps):
        columns = []
        for m in range(step * each, (step + 1) * each):
            mine, other = mine_ref[m], other_ref[m]
            columns.append(
                jnp.concatenate(
                    [jnp.where(core == 0, mine, other), jnp.where(core == 0, other, mine)], axis=0
                )
            )
        initial = jnp.concatenate(columns, axis=1)
        present = (initial[0:1] > 0.0).astype(jnp.float32)
        photo = jnp.concatenate(
            [photo_ref[first + m : first + m + 1, :] for m in range(step * each, (step + 1) * each)], axis=1
        )
        half_loss = jnp.concatenate([loss_ref[...]] * each, axis=1)
        source = jnp.concatenate([production_ref[...]] * each, axis=1) * photo
        current = initial
        for iteration in range(NEWTON):
            part_loss = half_loss * current
            moved = current - (initial + source) if iteration else -source
            misfit = moved - product(coupled_ref[...], current) + part_loss * current
            first_pass = product(precond_ref[...], misfit)
            second_pass = product(precond_ref[...], 2.0 * part_loss * first_pass)
            current = current - (first_pass - second_pass)
        result_ref[step] = (current * present)[:species]
        start = first * LANES + step * width
        copy = pltpu.make_async_copy(
            result_ref.at[step], out_ref.at[:, start : start + width], sems.at[step]
        )
        copy.start()
        copies.append(copy)
    for copy in copies:
        copy.wait()


def react(part, species, core, mine, other, photo, weights, so_far):
    blocks = mine.shape[0]
    steps = 2
    width = blocks * LANES // steps
    in_specs = [IN_SMEM] + [IN_VMEM] * 7
    operands = [core, mine, other, photo, *weights]
    aliases = {}
    if so_far is not None:
        in_specs.append(pl.BlockSpec(memory_space=pl.ANY))
        operands.append(so_far)
        aliases = {len(operands) - 1: 0}

    def kernel(*refs):
        react_kernel(part * blocks, *refs)

    return pl.pallas_call(
        kernel,
        out_shape=jax.ShapeDtypeStruct((species, blocks * PARTS * LANES), jnp.float32),
        in_specs=in_specs,
        out_specs=pl.BlockSpec(memory_space=pl.ANY),
        scratch_shapes=[
            pltpu.VMEM((steps, species, width), jnp.float32),
            pltpu.SemaphoreType.DMA((steps,)),
        ],
        input_output_aliases=aliases,
        compiler_params=pltpu.CompilerParams(vmem_limit_bytes=32 * 1024 * 1024),
        cost_estimate=pl.CostEstimate(
            flops=6 * 2 * 256 * 512 * blocks * LANES, bytes_accessed=8 * 1024 * 1024, transcendentals=0
        ),
        name="react",
    )(*operands)


def split(matrix):
    size = matrix.shape[0]
    padded = jnp.pad(matrix, ((0, ROWS - size), (0, ROWS - size)))
    high = lax.reduce_precision(padded, 8, 7)
    low = padded - high
    return jnp.concatenate([high, high, low], axis=1).astype(jnp.bfloat16)


def column(vector):
    return jnp.broadcast_to(jnp.pad(vector, (0, ROWS - vector.shape[0]))[:, None], (ROWS, LANES))


SWAP = ((0, 1), (1, 0))


def shards(
    conc, dest_tile, mixing_share, partner, photolysis, production, loss, rates, pattern, precond
):
    species, parcels = conc.shape
    devices = lax.axis_size("lat") * lax.axis_size("chip") * 2
    rows = mixing_share.shape[0] // LANES
    core = lax.axis_index("core").astype(jnp.int32)[None]

    def both_tiles(array):
        array = array.reshape(rows, LANES)
        other = lax.ppermute(array, "core", SWAP)
        return jnp.where(core[0] == 0, jnp.concatenate([array, other]), jnp.concatenate([other, array]))

    share, index = both_tiles(mixing_share), both_tiles(partner)
    photo = photolysis.reshape(rows, LANES)
    coupled = rates * jnp.kron(pattern.astype(jnp.float32), jnp.ones((SB, SB), jnp.float32))
    weights = (
        split(time_step * coupled),
        split(precond),
        column(time_step * production),
        column(time_step * loss),
    )
    packed = pack(conc, dest_tile.reshape(parcels // LANES, LANES), devices)
    packed = packed.reshape(devices, CHUNK // 4, 4, LANES)
    arrived = lax.all_to_all(
        packed, ("lat", "chip", "core"), split_axis=0, concat_axis=0, tiled=True
    ).reshape(devices * CHUNK, LANES)
    halves = [mix(part, core, arrived, share, index) for part in range(PARTS)]
    others = [lax.ppermute(give, "core", SWAP) for _, give in halves]
    result = None
    for part in range(PARTS):
        result = react(part, species, core, halves[part][0], others[part], photo, weights, result)
    return result


def solution(mesh):
    lat_count, lon_count = mesh.devices.shape
    by_core = Mesh(mesh.devices.reshape(lat_count, lon_count // 2, 2), ("lat", "chip", "core"))
    tiles = ("lat", "chip", "core")
    placed = (P(None, tiles), P(tiles, None), P(tiles), P(tiles), P(tiles), P(), P(), P(), P(), P())
    return jax.shard_map(
        shards, mesh=by_core, in_specs=placed, out_specs=P(None, tiles), check_vma=False
    )
```

```python
import jax
import jax.numpy as jnp
from jax import lax
from jax.experimental import pallas as pl
from jax.experimental.pallas import tpu as pltpu
from jax.sharding import Mesh
from jax.sharding import PartitionSpec as P

SB = 15
NEWTON = 2
time_step = 0.5

LANES = 128
CAP = 32
QUARTER = 20
HALF = 4 * QUARTER
ROWS = 2 * HALF
CHUNK = 3 * QUARTER
GROUP = 256
TOGETHER = 4
PARTS = 2
PIECES = 4


def regroup(parts):
    first, second, third, fourth = parts
    lane = lax.broadcasted_iota(jnp.int32, first.shape, 1)
    low_half = (lane & 64) == 0
    low_quarter = (lane & 32) == 0
    other_quarter = lane ^ 32

    def halves(a, b):
        moved = pltpu.roll(jnp.where(low_half, b, a), 64, 1)
        return jnp.where(low_half, a, moved), jnp.where(low_half, moved, b)

    def quarters(a, b):
        moved = jnp.take_along_axis(jnp.where(low_quarter, b, a), other_quarter, axis=1)
        return jnp.where(low_quarter, a, moved), jnp.where(low_quarter, moved, b)

    t0, t2 = halves(first, third)
    t1, t3 = halves(second, fourth)
    return (*quarters(t0, t1), *quarters(t2, t3))


def pack_kernel(conc_hbm, targets_hbm, out_hbm, out_ref, conc_ref, targets_ref, parts_ref, place_ref, group_ref, sums_ref, sems):
    species, parcels = conc_ref.shape
    read_conc = pltpu.make_async_copy(conc_hbm, conc_ref, sems.at[0])
    read_targets = pltpu.make_async_copy(targets_hbm, targets_ref, sems.at[1])
    read_targets.start()
    read_conc.start()
    read_targets.wait()
    row = lax.broadcasted_iota(jnp.int32, (LANES, LANES), 0)
    column = lax.broadcasted_iota(jnp.int32, (LANES, LANES), 1)
    earlier = (row < column).astype(jnp.float32).astype(jnp.bfloat16)
    sums_of = jnp.concatenate([earlier, jnp.ones((LANES, LANES), jnp.bfloat16)], axis=1)
    counted = jnp.zeros((LANES, LANES), jnp.float32)
    for block in range(parcels // LANES):
        span = slice(block * LANES, (block + 1) * LANES)
        targets = targets_ref[block : block + 1, :]
        onehot = (row == targets).astype(jnp.float32)
        sums = jnp.dot(onehot.astype(jnp.bfloat16), sums_of, preferred_element_type=jnp.float32)
        ranking = jnp.sum(onehot * (sums[:, :LANES] + counted), axis=0, keepdims=True)
        counted = counted + sums[:, LANES:]
        slot = targets * CAP + ranking.astype(jnp.int32)
        group_ref[:, span] = jnp.broadcast_to(slot // GROUP, (16, LANES))
        place = jnp.broadcast_to((slot % GROUP).astype(jnp.float32), (LANES, LANES))
        place = jnp.transpose(place).astype(jnp.int32)
        for side in range(GROUP // LANES):
            here = (place == column + side * LANES).astype(jnp.float32)
            place_ref[span, side * LANES : (side + 1) * LANES] = here.astype(jnp.bfloat16)
    read_conc.wait()
    conc = conc_ref[...]
    low = conc - conc.astype(jnp.bfloat16).astype(jnp.float32)
    filler = jnp.zeros((ROWS - species, parcels), jnp.float32)
    parts_ref[0:ROWS, :] = jnp.concatenate([conc, filler], axis=0).astype(jnp.bfloat16)
    parts_ref[ROWS:, :] = jnp.concatenate([low, filler], axis=0).astype(jnp.bfloat16)
    around = 16

    sent = TOGETHER * (GROUP // CAP) * CHUNK

    def write(i):
        rows = pl.ds(pl.multiple_of(i * sent, sent), sent)
        return pltpu.make_async_copy(out_ref.at[rows], out_hbm.at[rows], sems.at[2 + i])

    def step(i, carry):
        chosen = []
        for t in range(TOGETHER):
            mine = (group_ref[...] == i * TOGETHER + t).astype(jnp.float32).astype(jnp.bfloat16)
            chosen.append(parts_ref[...] * jnp.concatenate([mine] * (2 * ROWS // 16), axis=0))
        moved = jnp.dot(
            jnp.concatenate(chosen, axis=0), place_ref[...], preferred_element_type=jnp.float32
        )
        for t in range(TOGETHER):
            base = 2 * t * ROWS
            sums = moved[base : base + ROWS] + moved[base + ROWS : base + 2 * ROWS]
            for side in range(GROUP // LANES):
                sums_ref[t, side] = sums[:, side * LANES : (side + 1) * LANES]
        for t in range(TOGETHER):
            for side in range(GROUP // LANES):
                quad = (i * TOGETHER + t) * (GROUP // LANES) + side
                for half in range(2):
                    quarters = [
                        sums_ref[t, side, half * HALF + QUARTER * j : half * HALF + QUARTER * (j + 1), :]
                        for j in range(4)
                    ]
                    for d, chunk in enumerate(regroup(quarters)):
                        chip = quad * 2 + d // 2
                        to = (chip * 2 + half) * CHUNK + (d % 2) * QUARTER
                        out_ref[pl.ds(to, QUARTER), :] = chunk
                        if d % 2 == 0:
                            west = chip // around * around + (chip + around - 1) % around
                            to = (west * 2 + half) * CHUNK + 2 * QUARTER
                            out_ref[pl.ds(to, QUARTER), :] = chunk
        write(i).start()
        return carry

    lax.fori_loop(0, 16 // TOGETHER, step, 0)
    for i in range(16 // TOGETHER):
        write(i).wait()


IN_VMEM = pl.BlockSpec(memory_space=pltpu.VMEM)
IN_HBM = pl.BlockSpec(memory_space=pltpu.HBM)
IN_SMEM = pl.BlockSpec(memory_space=pltpu.SMEM)


def pack(conc, targets, devices):
    parcels = conc.shape[1]
    return pl.pallas_call(
        pack_kernel,
        out_shape=jax.ShapeDtypeStruct((devices * CHUNK, LANES), jnp.float32),
        in_specs=[IN_HBM, IN_HBM],
        out_specs=IN_HBM,
        scratch_shapes=[
            pltpu.VMEM((devices * CHUNK, LANES), jnp.float32),
            pltpu.VMEM(conc.shape, jnp.float32),
            pltpu.VMEM(targets.shape, jnp.int32),
            pltpu.VMEM((2 * ROWS, parcels), jnp.bfloat16),
            pltpu.VMEM((parcels, GROUP), jnp.bfloat16),
            pltpu.VMEM((16, parcels), jnp.int32),
            pltpu.VMEM((TOGETHER, GROUP // LANES, ROWS, LANES), jnp.float32),
            pltpu.SemaphoreType.DMA((2 + 16 // TOGETHER,)),
        ],
        compiler_params=pltpu.CompilerParams(vmem_limit_bytes=63 * 1024 * 1024),
        name="pack",
    )(conc, targets)


def mix_block(m, place, core, arrived_ref, share_ref, partner_ref, keep_ref, give_ref):
    tiles = []
    for tile in range(3):
        parts = []
        for s in range(4):
            start = (m * 4 + s) * CHUNK + tile * QUARTER
            parts.append(arrived_ref[pl.ds(start, QUARTER), :])
        tiles.append(regroup(parts))
    mixed = []
    for tile in range(2):
        own, east = tiles[tile], tiles[tile + 1]
        index = jnp.broadcast_to(partner_ref[tile, pl.ds(place, 1), :], (QUARTER, LANES))
        chosen = [jnp.take_along_axis(e, index, axis=1) for e in east]
        present = (own[0][0:1] > 0.0).astype(jnp.float32)
        alive = (chosen[0][0:1] > 0.0).astype(jnp.float32)
        weight = share_ref[tile, pl.ds(place, 1), :] * present * alive
        weight = jnp.broadcast_to(weight, (QUARTER, LANES))
        mixed.append([o + weight * (c - o) for o, c in zip(own, chosen)])
    for j in range(4):
        rows = slice(QUARTER * j, QUARTER * (j + 1))
        keep_ref[m, rows, :] = jnp.where(core == 0, mixed[0][j], mixed[1][j])
        give_ref[m, rows, :] = jnp.where(core == 0, mixed[1][j], mixed[0][j])


def mix_first_kernel(core_ref, arrived_hbm, share_ref, partner_ref, keep_ref, give_ref, rest_ref, land, sems):
    blocks = keep_ref.shape[0]
    each = blocks // PIECES
    length = each * 4 * CHUNK
    core = core_ref[0]
    reads = []
    for piece in range(PIECES):
        rows = slice(piece * length, (piece + 1) * length)
        reads.append(pltpu.make_async_copy(arrived_hbm.at[rows], land.at[rows], sems.at[piece]))
    rest = pltpu.make_async_copy(
        arrived_hbm.at[PIECES * length : 2 * PIECES * length], rest_ref, sems.at[PIECES]
    )
    for read in (*reads, rest):
        read.start()
    for piece in range(PIECES):
        reads[piece].wait()

        def body(m, carry):
            mix_block(m, m, core, land, share_ref, partner_ref, keep_ref, give_ref)
            return carry

        lax.fori_loop(piece * each, (piece + 1) * each, body, 0, unroll=2)
    rest.wait()


def mix_second_kernel(core_ref, rest_ref, share_ref, partner_ref, keep_ref, give_ref):
    blocks = keep_ref.shape[0]
    core = core_ref[0]

    def body(m, carry):
        mix_block(m, blocks + m, core, rest_ref, share_ref, partner_ref, keep_ref, give_ref)
        return carry

    lax.fori_loop(0, blocks, body, 0, unroll=2)


def mix(core, arrived, share, partner):
    half = arrived.shape[0] // 2
    blocks = half // (4 * CHUNK)
    shape = jax.ShapeDtypeStruct((blocks, HALF, LANES), jnp.float32)
    params = pltpu.CompilerParams(vmem_limit_bytes=8 * 1024 * 1024)
    cost = pl.CostEstimate(flops=0, bytes_accessed=8 * 1024 * 1024, transcendentals=0)
    rest_shape = jax.ShapeDtypeStruct((half, LANES), jnp.float32)
    keep, give, rest = pl.pallas_call(
        mix_first_kernel,
        out_shape=(shape, shape, rest_shape),
        in_specs=[IN_SMEM, IN_HBM, IN_VMEM, IN_VMEM],
        out_specs=(IN_VMEM, IN_VMEM, IN_VMEM),
        scratch_shapes=[
            pltpu.VMEM((half, LANES), jnp.float32),
            pltpu.SemaphoreType.DMA((PIECES + 1,)),
        ],
        compiler_params=params,
        cost_estimate=cost,
        name="mix_first",
    )(core, arrived, share, partner)
    second = pl.pallas_call(
        mix_second_kernel,
        out_shape=(shape, shape),
        in_specs=[IN_SMEM, IN_VMEM, IN_VMEM, IN_VMEM],
        out_specs=(IN_VMEM, IN_VMEM),
        compiler_params=params,
        cost_estimate=cost,
        name="mix_second",
    )(core, rest, share, partner)
    return (keep, give), second


def product(weights, value):
    high = value.astype(jnp.bfloat16)
    low = (value - high.astype(jnp.float32)).astype(jnp.bfloat16)
    return jnp.dot(
        weights,
        jnp.concatenate([high, low, high], axis=0),
        preferred_element_type=jnp.float32,
    )


def react_kernel(
    first, core_ref, mine_ref, other_ref, photo_ref, coupled_ref, precond_ref, production_ref, loss_ref, *rest
):
    out_ref, result_ref, sems = rest[-3:]
    blocks = mine_ref.shape[0]
    steps = result_ref.shape[0]
    each = blocks // steps
    width = each * LANES
    species = out_ref.shape[0]
    core = core_ref[0]
    copies = []
    for step in range(steps):
        columns = []
        for m in range(step * each, (step + 1) * each):
            mine, other = mine_ref[m], other_ref[m]
            columns.append(
                jnp.concatenate(
                    [jnp.where(core == 0, mine, other), jnp.where(core == 0, other, mine)], axis=0
                )
            )
        initial = jnp.concatenate(columns, axis=1)
        present = (initial[0:1] > 0.0).astype(jnp.float32)
        photo = jnp.concatenate(
            [photo_ref[first + m : first + m + 1, :] for m in range(step * each, (step + 1) * each)], axis=1
        )
        half_loss = jnp.concatenate([loss_ref[...]] * each, axis=1)
        source = jnp.concatenate([production_ref[...]] * each, axis=1) * photo
        current = initial
        for iteration in range(NEWTON):
            part_loss = half_loss * current
            moved = current - (initial + source) if iteration else -source
            misfit = moved - product(coupled_ref[...], current) + part_loss * current
            first_pass = product(precond_ref[...], misfit)
            second_pass = product(precond_ref[...], 2.0 * part_loss * first_pass)
            current = current - (first_pass - second_pass)
        result_ref[step] = (current * present)[:species]
        start = first * LANES + step * width
        copy = pltpu.make_async_copy(
            result_ref.at[step], out_ref.at[:, start : start + width], sems.at[step]
        )
        copy.start()
        copies.append(copy)
    for copy in copies:
        copy.wait()


def react(part, species, core, mine, other, photo, weights, so_far):
    blocks = mine.shape[0]
    steps = 2
    width = blocks * LANES // steps
    in_specs = [IN_SMEM] + [IN_VMEM] * 7
    operands = [core, mine, other, photo, *weights]
    aliases = {}
    if so_far is not None:
        in_specs.append(pl.BlockSpec(memory_space=pl.ANY))
        operands.append(so_far)
        aliases = {len(operands) - 1: 0}

    def kernel(*refs):
        react_kernel(part * blocks, *refs)

    return pl.pallas_call(
        kernel,
        out_shape=jax.ShapeDtypeStruct((species, blocks * PARTS * LANES), jnp.float32),
        in_specs=in_specs,
        out_specs=pl.BlockSpec(memory_space=pl.ANY),
        scratch_shapes=[
            pltpu.VMEM((steps, species, width), jnp.float32),
            pltpu.SemaphoreType.DMA((steps,)),
        ],
        input_output_aliases=aliases,
        compiler_params=pltpu.CompilerParams(vmem_limit_bytes=16 * 1024 * 1024),
        cost_estimate=pl.CostEstimate(
            flops=6 * 2 * 256 * 512 * blocks * LANES, bytes_accessed=8 * 1024 * 1024, transcendentals=0
        ),
        name="react",
    )(*operands)


def split(matrix):
    size = matrix.shape[0]
    padded = jnp.pad(matrix, ((0, ROWS - size), (0, ROWS - size)))
    high = lax.reduce_precision(padded, 8, 7)
    low = padded - high
    return jnp.concatenate([high, high, low], axis=1).astype(jnp.bfloat16)


def column(vector):
    return jnp.broadcast_to(jnp.pad(vector, (0, ROWS - vector.shape[0]))[:, None], (ROWS, LANES))


SWAP = ((0, 1), (1, 0))


def shards(
    conc, dest_tile, mixing_share, partner, photolysis, production, loss, rates, pattern, precond
):
    species, parcels = conc.shape
    devices = lax.axis_size("lat") * lax.axis_size("chip") * 2
    rows = mixing_share.shape[0] // LANES
    core = lax.axis_index("core").astype(jnp.int32)[None]

    def both_tiles(array):
        array = array.reshape(rows, LANES)
        other = lax.ppermute(array, "core", SWAP)
        return jnp.where(core[0] == 0, jnp.stack([array, other]), jnp.stack([other, array]))

    share, index = both_tiles(mixing_share), both_tiles(partner)
    photo = photolysis.reshape(rows, LANES)
    coupled = rates * jnp.kron(pattern.astype(jnp.float32), jnp.ones((SB, SB), jnp.float32))
    weights = (
        split(time_step * coupled),
        split(precond),
        column(time_step * production),
        column(time_step * loss),
    )
    packed = pack(conc, dest_tile.reshape(parcels // LANES, LANES), devices)
    packed = packed.reshape(devices, CHUNK // 4, 4, LANES)
    arrived = lax.all_to_all(
        packed, ("lat", "chip", "core"), split_axis=0, concat_axis=0, tiled=True
    ).reshape(devices * CHUNK, LANES)
    arrived, share, index, photo, *weights = lax.optimization_barrier(
        (arrived, share, index, photo, *weights)
    )
    halves = mix(core, arrived, share, index)
    others = [lax.ppermute(give, "core", SWAP) for _, give in halves]
    result = None
    for part in range(PARTS):
        result = react(part, species, core, halves[part][0], others[part], photo, weights, result)
    return result


def solution(mesh):
    lat_count, lon_count = mesh.devices.shape
    by_core = Mesh(mesh.devices.reshape(lat_count, lon_count // 2, 2), ("lat", "chip", "core"))
    tiles = ("lat", "chip", "core")
    placed = (P(None, tiles), P(tiles, None), P(tiles), P(tiles), P(tiles), P(), P(), P(), P(), P())
    return jax.shard_map(
        shards, mesh=by_core, in_specs=placed, out_specs=P(None, tiles), check_vma=False
    )
```

```python
import jax
import jax.numpy as jnp
from jax import lax
from jax.experimental import pallas as pl
from jax.experimental.pallas import tpu as pltpu
from jax.sharding import Mesh
from jax.sharding import PartitionSpec as P

SB = 15
NEWTON = 2
time_step = 0.5

LANES = 128
CAP = 32
QUARTER = 19
HALF = 4 * QUARTER
SENT = 2 * HALF
BLOCK = 80
ROWS = 2 * BLOCK
CHUNK = 3 * QUARTER
GROUP = 256
TOGETHER = 4
PARTS = 2
PIECES = 4


def regroup(parts):
    first, second, third, fourth = parts
    lane = lax.broadcasted_iota(jnp.int32, first.shape, 1)
    low_half = (lane & 64) == 0
    low_quarter = (lane & 32) == 0
    other_quarter = lane ^ 32

    def halves(a, b):
        moved = pltpu.roll(jnp.where(low_half, b, a), 64, 1)
        return jnp.where(low_half, a, moved), jnp.where(low_half, moved, b)

    def quarters(a, b):
        moved = jnp.take_along_axis(jnp.where(low_quarter, b, a), other_quarter, axis=1)
        return jnp.where(low_quarter, a, moved), jnp.where(low_quarter, moved, b)

    t0, t2 = halves(first, third)
    t1, t3 = halves(second, fourth)
    return (*quarters(t0, t1), *quarters(t2, t3))


def pack_kernel(conc_hbm, targets_hbm, out_hbm, out_ref, conc_ref, targets_ref, parts_ref, place_ref, group_ref, sums_ref, sems):
    species, parcels = conc_ref.shape
    read_conc = pltpu.make_async_copy(conc_hbm, conc_ref, sems.at[0])
    read_targets = pltpu.make_async_copy(targets_hbm, targets_ref, sems.at[1])
    read_targets.start()
    read_conc.start()
    read_targets.wait()
    row = lax.broadcasted_iota(jnp.int32, (LANES, LANES), 0)
    column = lax.broadcasted_iota(jnp.int32, (LANES, LANES), 1)
    earlier = (row < column).astype(jnp.float32).astype(jnp.bfloat16)
    sums_of = jnp.concatenate([earlier, jnp.ones((LANES, LANES), jnp.bfloat16)], axis=1)
    counted = jnp.zeros((LANES, LANES), jnp.float32)
    for block in range(parcels // LANES):
        span = slice(block * LANES, (block + 1) * LANES)
        targets = targets_ref[block : block + 1, :]
        onehot = (row == targets).astype(jnp.float32)
        sums = jnp.dot(onehot.astype(jnp.bfloat16), sums_of, preferred_element_type=jnp.float32)
        ranking = jnp.sum(onehot * (sums[:, :LANES] + counted), axis=0, keepdims=True)
        counted = counted + sums[:, LANES:]
        slot = targets * CAP + ranking.astype(jnp.int32)
        group_ref[:, span] = jnp.broadcast_to(slot // GROUP, (16, LANES))
        place = jnp.broadcast_to((slot % GROUP).astype(jnp.float32), (LANES, LANES))
        place = jnp.transpose(place).astype(jnp.int32)
        for side in range(GROUP // LANES):
            here = (place == column + side * LANES).astype(jnp.float32)
            place_ref[span, side * LANES : (side + 1) * LANES] = here.astype(jnp.bfloat16)
    read_conc.wait()
    conc = conc_ref[...]
    low = conc - conc.astype(jnp.bfloat16).astype(jnp.float32)
    filler = jnp.zeros((SENT - species, parcels), jnp.float32)
    parts_ref[...] = jnp.concatenate([conc, filler, low, filler], axis=0).astype(jnp.bfloat16)
    around = 16

    sent = TOGETHER * (GROUP // CAP) * CHUNK

    def write(i):
        rows = pl.ds(pl.multiple_of(i * sent, sent), sent)
        return pltpu.make_async_copy(out_ref.at[rows], out_hbm.at[rows], sems.at[2 + i])

    def step(i, carry):
        chosen = []
        for t in range(TOGETHER):
            mine = (group_ref[...] == i * TOGETHER + t).astype(jnp.float32).astype(jnp.bfloat16)
            chosen.append(parts_ref[...] * jnp.concatenate([mine] * (2 * SENT // 16), axis=0))
        moved = jnp.dot(
            jnp.concatenate(chosen, axis=0), place_ref[...], preferred_element_type=jnp.float32
        )
        for t in range(TOGETHER):
            base = 2 * t * SENT
            sums = moved[base : base + SENT] + moved[base + SENT : base + 2 * SENT]
            for side in range(GROUP // LANES):
                sums_ref[t, side] = sums[:, side * LANES : (side + 1) * LANES]
        for t in range(TOGETHER):
            for side in range(GROUP // LANES):
                quad = (i * TOGETHER + t) * (GROUP // LANES) + side
                for half in range(2):
                    quarters = [
                        sums_ref[t, side, half * HALF + QUARTER * j : half * HALF + QUARTER * (j + 1), :]
                        for j in range(4)
                    ]
                    for d, chunk in enumerate(regroup(quarters)):
                        chip = quad * 2 + d // 2
                        to = (chip * 2 + half) * CHUNK + (d % 2) * QUARTER
                        out_ref[pl.ds(to, QUARTER), :] = chunk
                        if d % 2 == 0:
                            west = chip // around * around + (chip + around - 1) % around
                            to = (west * 2 + half) * CHUNK + 2 * QUARTER
                            out_ref[pl.ds(to, QUARTER), :] = chunk
        write(i).start()
        return carry

    lax.fori_loop(0, 16 // TOGETHER, step, 0)
    for i in range(16 // TOGETHER):
        write(i).wait()


IN_VMEM = pl.BlockSpec(memory_space=pltpu.VMEM)
IN_HBM = pl.BlockSpec(memory_space=pltpu.HBM)
IN_SMEM = pl.BlockSpec(memory_space=pltpu.SMEM)


def pack(conc, targets, devices):
    parcels = conc.shape[1]
    return pl.pallas_call(
        pack_kernel,
        out_shape=jax.ShapeDtypeStruct((devices * CHUNK, LANES), jnp.float32),
        in_specs=[IN_HBM, IN_HBM],
        out_specs=IN_HBM,
        scratch_shapes=[
            pltpu.VMEM((devices * CHUNK, LANES), jnp.float32),
            pltpu.VMEM(conc.shape, jnp.float32),
            pltpu.VMEM(targets.shape, jnp.int32),
            pltpu.VMEM((2 * SENT, parcels), jnp.bfloat16),
            pltpu.VMEM((parcels, GROUP), jnp.bfloat16),
            pltpu.VMEM((16, parcels), jnp.int32),
            pltpu.VMEM((TOGETHER, GROUP // LANES, SENT, LANES), jnp.float32),
            pltpu.SemaphoreType.DMA((2 + 16 // TOGETHER,)),
        ],
        compiler_params=pltpu.CompilerParams(vmem_limit_bytes=63 * 1024 * 1024),
        name="pack",
    )(conc, targets)


def mix_block(m, place, core, arrived_ref, share_ref, partner_ref, keep_ref, give_ref):
    tiles = []
    for tile in range(3):
        parts = []
        for s in range(4):
            start = (m * 4 + s) * CHUNK + tile * QUARTER
            parts.append(arrived_ref[pl.ds(start, QUARTER), :])
        tiles.append(regroup(parts))
    mixed = []
    for tile in range(2):
        own, east = tiles[tile], tiles[tile + 1]
        index = jnp.broadcast_to(partner_ref[tile, pl.ds(place, 1), :], (QUARTER, LANES))
        chosen = [jnp.take_along_axis(e, index, axis=1) for e in east]
        present = (own[0][0:1] > 0.0).astype(jnp.float32)
        alive = (chosen[0][0:1] > 0.0).astype(jnp.float32)
        weight = share_ref[tile, pl.ds(place, 1), :] * present * alive
        weight = jnp.broadcast_to(weight, (QUARTER, LANES))
        mixed.append([o + weight * (c - o) for o, c in zip(own, chosen)])
    for j in range(4):
        rows = slice(QUARTER * j, QUARTER * (j + 1))
        keep_ref[m, rows, :] = jnp.where(core == 0, mixed[0][j], mixed[1][j])
        give_ref[m, rows, :] = jnp.where(core == 0, mixed[1][j], mixed[0][j])
    empty = jnp.zeros((BLOCK - HALF, LANES), jnp.float32)
    keep_ref[m, HALF:, :] = empty
    give_ref[m, HALF:, :] = empty


def mix_first_kernel(core_ref, arrived_hbm, share_ref, partner_ref, keep_ref, give_ref, rest_ref, land, sems):
    blocks = keep_ref.shape[0]
    each = blocks // PIECES
    length = each * 4 * CHUNK
    core = core_ref[0]
    reads = []
    for piece in range(PIECES):
        rows = slice(piece * length, (piece + 1) * length)
        reads.append(pltpu.make_async_copy(arrived_hbm.at[rows], land.at[rows], sems.at[piece]))
    rest = pltpu.make_async_copy(
        arrived_hbm.at[PIECES * length : 2 * PIECES * length], rest_ref, sems.at[PIECES]
    )
    for read in (*reads, rest):
        read.start()
    for piece in range(PIECES):
        reads[piece].wait()

        def body(m, carry):
            mix_block(m, m, core, land, share_ref, partner_ref, keep_ref, give_ref)
            return carry

        lax.fori_loop(piece * each, (piece + 1) * each, body, 0, unroll=2)
    rest.wait()


def mix_second_kernel(core_ref, rest_ref, share_ref, partner_ref, keep_ref, give_ref):
    blocks = keep_ref.shape[0]
    core = core_ref[0]

    def body(m, carry):
        mix_block(m, blocks + m, core, rest_ref, share_ref, partner_ref, keep_ref, give_ref)
        return carry

    lax.fori_loop(0, blocks, body, 0, unroll=2)


def mix(core, arrived, share, partner):
    half = arrived.shape[0] // 2
    blocks = half // (4 * CHUNK)
    shape = jax.ShapeDtypeStruct((blocks, BLOCK, LANES), jnp.float32)
    params = pltpu.CompilerParams(vmem_limit_bytes=8 * 1024 * 1024)
    cost = pl.CostEstimate(flops=0, bytes_accessed=8 * 1024 * 1024, transcendentals=0)
    rest_shape = jax.ShapeDtypeStruct((half, LANES), jnp.float32)
    keep, give, rest = pl.pallas_call(
        mix_first_kernel,
        out_shape=(shape, shape, rest_shape),
        in_specs=[IN_SMEM, IN_HBM, IN_VMEM, IN_VMEM],
        out_specs=(IN_VMEM, IN_VMEM, IN_VMEM),
        scratch_shapes=[
            pltpu.VMEM((half, LANES), jnp.float32),
            pltpu.SemaphoreType.DMA((PIECES + 1,)),
        ],
        compiler_params=params,
        cost_estimate=cost,
        name="mix_first",
    )(core, arrived, share, partner)
    second = pl.pallas_call(
        mix_second_kernel,
        out_shape=(shape, shape),
        in_specs=[IN_SMEM, IN_VMEM, IN_VMEM, IN_VMEM],
        out_specs=(IN_VMEM, IN_VMEM),
        compiler_params=params,
        cost_estimate=cost,
        name="mix_second",
    )(core, rest, share, partner)
    return (keep, give), second


def product(weights, value):
    high = value.astype(jnp.bfloat16)
    low = (value - high.astype(jnp.float32)).astype(jnp.bfloat16)
    return jnp.dot(
        weights,
        jnp.concatenate([high, low, high], axis=0),
        preferred_element_type=jnp.float32,
    )


def react_kernel(
    first, core_ref, mine_ref, other_ref, photo_ref, coupled_ref, precond_ref, production_ref, loss_ref, *rest
):
    out_ref, result_ref, sems = rest[-3:]
    blocks = mine_ref.shape[0]
    steps = result_ref.shape[0]
    each = blocks // steps
    width = each * LANES
    species = out_ref.shape[0]
    core = core_ref[0]
    copies = []
    for step in range(steps):
        columns = []
        for m in range(step * each, (step + 1) * each):
            mine, other = mine_ref[m], other_ref[m]
            columns.append(
                jnp.concatenate(
                    [jnp.where(core == 0, mine, other), jnp.where(core == 0, other, mine)], axis=0
                )
            )
        initial = jnp.concatenate(columns, axis=1)
        present = (initial[0:1] > 0.0).astype(jnp.float32)
        photo = jnp.concatenate(
            [photo_ref[first + m : first + m + 1, :] for m in range(step * each, (step + 1) * each)], axis=1
        )
        half_loss = jnp.concatenate([loss_ref[...]] * each, axis=1)
        source = jnp.concatenate([production_ref[...]] * each, axis=1) * photo
        current = initial
        for iteration in range(NEWTON):
            part_loss = half_loss * current
            moved = current - (initial + source) if iteration else -source
            misfit = moved - product(coupled_ref[...], current) + part_loss * current
            first_pass = product(precond_ref[...], misfit)
            second_pass = product(precond_ref[...], 2.0 * part_loss * first_pass)
            current = current - (first_pass - second_pass)
        result = current * present
        result_ref[step, :HALF] = result[:HALF]
        result_ref[step, HALF:] = result[BLOCK : BLOCK + species - HALF]
        start = first * LANES + step * width
        copy = pltpu.make_async_copy(
            result_ref.at[step], out_ref.at[:, start : start + width], sems.at[step]
        )
        copy.start()
        copies.append(copy)
    for copy in copies:
        copy.wait()


def react(part, species, core, mine, other, photo, weights, so_far):
    blocks = mine.shape[0]
    steps = 2
    width = blocks * LANES // steps
    in_specs = [IN_SMEM] + [IN_VMEM] * 7
    operands = [core, mine, other, photo, *weights]
    aliases = {}
    if so_far is not None:
        in_specs.append(pl.BlockSpec(memory_space=pl.ANY))
        operands.append(so_far)
        aliases = {len(operands) - 1: 0}

    def kernel(*refs):
        react_kernel(part * blocks, *refs)

    return pl.pallas_call(
        kernel,
        out_shape=jax.ShapeDtypeStruct((species, blocks * PARTS * LANES), jnp.float32),
        in_specs=in_specs,
        out_specs=pl.BlockSpec(memory_space=pl.ANY),
        scratch_shapes=[
            pltpu.VMEM((steps, species, width), jnp.float32),
            pltpu.SemaphoreType.DMA((steps,)),
        ],
        input_output_aliases=aliases,
        compiler_params=pltpu.CompilerParams(vmem_limit_bytes=16 * 1024 * 1024),
        cost_estimate=pl.CostEstimate(
            flops=6 * 2 * 256 * 512 * blocks * LANES, bytes_accessed=8 * 1024 * 1024, transcendentals=0
        ),
        name="react",
    )(*operands)


def spread(array, axis):
    gaps = [(0, 0)] * array.ndim
    first, second = jnp.split(array, [HALF], axis=axis)
    gaps[axis] = (0, BLOCK - first.shape[axis])
    first = jnp.pad(first, gaps)
    gaps[axis] = (0, BLOCK - second.shape[axis])
    return jnp.concatenate([first, jnp.pad(second, gaps)], axis=axis)


def split(matrix):
    padded = spread(spread(matrix, 0), 1)
    high = lax.reduce_precision(padded, 8, 7)
    low = padded - high
    return jnp.concatenate([high, high, low], axis=1).astype(jnp.bfloat16)


def column(vector):
    return jnp.broadcast_to(spread(vector, 0)[:, None], (ROWS, LANES))


SWAP = ((0, 1), (1, 0))


def shards(
    conc, dest_tile, mixing_share, partner, photolysis, production, loss, rates, pattern, precond
):
    species, parcels = conc.shape
    devices = lax.axis_size("lat") * lax.axis_size("chip") * 2
    rows = mixing_share.shape[0] // LANES
    core = lax.axis_index("core").astype(jnp.int32)[None]

    def both_tiles(array):
        array = array.reshape(rows, LANES)
        other = lax.ppermute(array, "core", SWAP)
        return jnp.where(core[0] == 0, jnp.stack([array, other]), jnp.stack([other, array]))

    share, index = both_tiles(mixing_share), both_tiles(partner)
    photo = photolysis.reshape(rows, LANES)
    coupled = rates * jnp.kron(pattern.astype(jnp.float32), jnp.ones((SB, SB), jnp.float32))
    weights = (
        split(time_step * coupled),
        split(precond),
        column(time_step * production),
        column(time_step * loss),
    )
    packed = pack(conc, dest_tile.reshape(parcels // LANES, LANES), devices)
    packed = packed.reshape(devices, CHUNK, 1, LANES)
    arrived = lax.all_to_all(
        packed, ("lat", "chip", "core"), split_axis=0, concat_axis=0, tiled=True
    ).reshape(devices * CHUNK, LANES)
    arrived, share, index, photo, *weights = lax.optimization_barrier(
        (arrived, share, index, photo, *weights)
    )
    halves = mix(core, arrived, share, index)
    others = [lax.ppermute(give, "core", SWAP) for _, give in halves]
    result = None
    for part in range(PARTS):
        result = react(part, species, core, halves[part][0], others[part], photo, weights, result)
    return result


def solution(mesh):
    lat_count, lon_count = mesh.devices.shape
    by_core = Mesh(mesh.devices.reshape(lat_count, lon_count // 2, 2), ("lat", "chip", "core"))
    tiles = ("lat", "chip", "core")
    placed = (P(None, tiles), P(tiles, None), P(tiles), P(tiles), P(tiles), P(), P(), P(), P(), P())
    return jax.shard_map(
        shards, mesh=by_core, in_specs=placed, out_specs=P(None, tiles), check_vma=False
    )
```

```python
import jax
import jax.numpy as jnp
from jax import lax
from jax.experimental import pallas as pl
from jax.experimental.pallas import tpu as pltpu
from jax.sharding import Mesh
from jax.sharding import PartitionSpec as P

SB = 15
NEWTON = 2
time_step = 0.5

LANES = 128
CAP = 32
QUARTER = 19
HALF = 4 * QUARTER
SENT = 2 * HALF
BLOCK = 80
ROWS = 2 * BLOCK
CHUNK = 3 * QUARTER
GROUP = 256
TOGETHER = 2
PARTS = 2
PIECES = 8


def regroup(parts):
    first, second, third, fourth = parts
    lane = lax.broadcasted_iota(jnp.int32, first.shape, 1)
    low_half = (lane & 64) == 0
    low_quarter = (lane & 32) == 0
    other_quarter = lane ^ 32

    def halves(a, b):
        moved = pltpu.roll(jnp.where(low_half, b, a), 64, 1)
        return jnp.where(low_half, a, moved), jnp.where(low_half, moved, b)

    def quarters(a, b):
        moved = jnp.take_along_axis(jnp.where(low_quarter, b, a), other_quarter, axis=1)
        return jnp.where(low_quarter, a, moved), jnp.where(low_quarter, moved, b)

    t0, t2 = halves(first, third)
    t1, t3 = halves(second, fourth)
    return (*quarters(t0, t1), *quarters(t2, t3))


def pack_kernel(conc_hbm, targets_hbm, out_hbm, out_ref, conc_ref, targets_ref, parts_ref, place_ref, group_ref, sums_ref, sems):
    species, parcels = conc_ref.shape
    read_conc = pltpu.make_async_copy(conc_hbm, conc_ref, sems.at[0])
    read_targets = pltpu.make_async_copy(targets_hbm, targets_ref, sems.at[1])
    read_targets.start()
    read_conc.start()
    read_targets.wait()
    row = lax.broadcasted_iota(jnp.int32, (LANES, LANES), 0)
    column = lax.broadcasted_iota(jnp.int32, (LANES, LANES), 1)
    earlier = (row < column).astype(jnp.float32).astype(jnp.bfloat16)
    sums_of = jnp.concatenate([earlier, jnp.ones((LANES, LANES), jnp.bfloat16)], axis=1)
    counted = jnp.zeros((LANES, LANES), jnp.float32)
    for block in range(parcels // LANES):
        span = slice(block * LANES, (block + 1) * LANES)
        targets = targets_ref[block : block + 1, :]
        onehot = (row == targets).astype(jnp.float32)
        sums = jnp.dot(onehot.astype(jnp.bfloat16), sums_of, preferred_element_type=jnp.float32)
        ranking = jnp.sum(onehot * (sums[:, :LANES] + counted), axis=0, keepdims=True)
        counted = counted + sums[:, LANES:]
        slot = targets * CAP + ranking.astype(jnp.int32)
        group_ref[:, span] = jnp.broadcast_to(slot // GROUP, (16, LANES))
        place = jnp.broadcast_to((slot % GROUP).astype(jnp.float32), (LANES, LANES))
        place = jnp.transpose(place).astype(jnp.int32)
        for side in range(GROUP // LANES):
            here = (place == column + side * LANES).astype(jnp.float32)
            place_ref[span, side * LANES : (side + 1) * LANES] = here.astype(jnp.bfloat16)
    read_conc.wait()
    conc = conc_ref[...]
    low = conc - conc.astype(jnp.bfloat16).astype(jnp.float32)
    filler = jnp.zeros((SENT - species, parcels), jnp.float32)
    parts_ref[...] = jnp.concatenate([conc, filler, low, filler], axis=0).astype(jnp.bfloat16)
    around = 16

    sent = around * 2 * CHUNK
    per_lat = around * 2 * CAP // GROUP

    def write(i):
        rows = slice(i * sent, (i + 1) * sent)
        return pltpu.make_async_copy(out_ref.at[rows], out_hbm.at[rows], sems.at[2 + i])

    def move(i):
        chosen = []
        for t in range(TOGETHER):
            mine = (group_ref[...] == i * TOGETHER + t).astype(jnp.float32).astype(jnp.bfloat16)
            chosen.append(parts_ref[...] * jnp.concatenate([mine] * (2 * SENT // 16), axis=0))
        return jnp.dot(
            jnp.concatenate(chosen, axis=0), place_ref[...], preferred_element_type=jnp.float32
        )

    def arrange(i, moved):
        for t in range(TOGETHER):
            base = 2 * t * SENT
            sums = moved[base : base + SENT] + moved[base + SENT : base + 2 * SENT]
            for side in range(GROUP // LANES):
                sums_ref[i % 2, t, side] = sums[:, side * LANES : (side + 1) * LANES]
        for t in range(TOGETHER):
            for side in range(GROUP // LANES):
                quad = (i * TOGETHER + t) * (GROUP // LANES) + side
                for half in range(2):
                    quarters = [
                        sums_ref[i % 2, t, side, half * HALF + QUARTER * j : half * HALF + QUARTER * (j + 1), :]
                        for j in range(4)
                    ]
                    for d, chunk in enumerate(regroup(quarters)):
                        chip = quad * 2 + d // 2
                        to = (chip * 2 + half) * CHUNK + (d % 2) * QUARTER
                        out_ref[to : to + QUARTER, :] = chunk
                        if d % 2 == 0:
                            west = chip // around * around + (chip + around - 1) % around
                            to = (west * 2 + half) * CHUNK + 2 * QUARTER
                            out_ref[to : to + QUARTER, :] = chunk
            if (i * TOGETHER + t + 1) % per_lat == 0:
                write((i * TOGETHER + t) // per_lat).start()

    steps = parcels * 2 // GROUP // TOGETHER
    for i in range(steps):
        arrange(i, move(i))
    for i in range(out_ref.shape[0] // sent):
        write(i).wait()


IN_VMEM = pl.BlockSpec(memory_space=pltpu.VMEM)
IN_HBM = pl.BlockSpec(memory_space=pltpu.HBM)
IN_SMEM = pl.BlockSpec(memory_space=pltpu.SMEM)


def pack(conc, targets, devices):
    parcels = conc.shape[1]
    return pl.pallas_call(
        pack_kernel,
        out_shape=jax.ShapeDtypeStruct((devices * CHUNK, LANES), jnp.float32),
        in_specs=[IN_HBM, IN_HBM],
        out_specs=IN_HBM,
        scratch_shapes=[
            pltpu.VMEM((devices * CHUNK, LANES), jnp.float32),
            pltpu.VMEM(conc.shape, jnp.float32),
            pltpu.VMEM(targets.shape, jnp.int32),
            pltpu.VMEM((2 * SENT, parcels), jnp.bfloat16),
            pltpu.VMEM((parcels, GROUP), jnp.bfloat16),
            pltpu.VMEM((16, parcels), jnp.int32),
            pltpu.VMEM((2, TOGETHER, GROUP // LANES, SENT, LANES), jnp.float32),
            pltpu.SemaphoreType.DMA((2 + 4,)),
        ],
        compiler_params=pltpu.CompilerParams(vmem_limit_bytes=63 * 1024 * 1024),
        name="pack",
    )(conc, targets)


def mix_block(m, place, core, arrived_ref, share_ref, partner_ref, keep_ref, give_ref):
    tiles = []
    for tile in range(3):
        parts = []
        for s in range(4):
            start = (m * 4 + s) * CHUNK + tile * QUARTER
            parts.append(arrived_ref[pl.ds(start, QUARTER), :])
        tiles.append(regroup(parts))
    mixed = []
    for tile in range(2):
        own, east = tiles[tile], tiles[tile + 1]
        index = jnp.broadcast_to(partner_ref[tile, pl.ds(place, 1), :], (QUARTER, LANES))
        chosen = [jnp.take_along_axis(e, index, axis=1) for e in east]
        present = (own[0][0:1] > 0.0).astype(jnp.float32)
        alive = (chosen[0][0:1] > 0.0).astype(jnp.float32)
        weight = share_ref[tile, pl.ds(place, 1), :] * present * alive
        weight = jnp.broadcast_to(weight, (QUARTER, LANES))
        mixed.append([o + weight * (c - o) for o, c in zip(own, chosen)])
    for j in range(4):
        rows = slice(QUARTER * j, QUARTER * (j + 1))
        keep_ref[m, rows, :] = jnp.where(core == 0, mixed[0][j], mixed[1][j])
        give_ref[m, rows, :] = jnp.where(core == 0, mixed[1][j], mixed[0][j])
    empty = jnp.zeros((BLOCK - HALF, LANES), jnp.float32)
    keep_ref[m, HALF:, :] = empty
    give_ref[m, HALF:, :] = empty


def mix_first_kernel(core_ref, arrived_hbm, share_ref, partner_ref, keep_ref, give_ref, rest_ref, land, sems):
    blocks = keep_ref.shape[0]
    each = blocks // PIECES
    length = each * 4 * CHUNK
    core = core_ref[0]
    reads = []
    for piece in range(PIECES):
        rows = slice(piece * length, (piece + 1) * length)
        reads.append(pltpu.make_async_copy(arrived_hbm.at[rows], land.at[rows], sems.at[piece]))
    rest = pltpu.make_async_copy(
        arrived_hbm.at[PIECES * length : 2 * PIECES * length], rest_ref, sems.at[PIECES]
    )
    for read in (*reads, rest):
        read.start()
    for piece in range(PIECES):
        reads[piece].wait()

        def body(m, carry):
            mix_block(m, m, core, land, share_ref, partner_ref, keep_ref, give_ref)
            return carry

        lax.fori_loop(piece * each, (piece + 1) * each, body, 0, unroll=2)
    rest.wait()


def mix_second_kernel(core_ref, rest_ref, share_ref, partner_ref, keep_ref, give_ref):
    blocks = keep_ref.shape[0]
    core = core_ref[0]

    def body(m, carry):
        mix_block(m, blocks + m, core, rest_ref, share_ref, partner_ref, keep_ref, give_ref)
        return carry

    lax.fori_loop(0, blocks, body, 0, unroll=2)


def mix(core, arrived, share, partner):
    half = arrived.shape[0] // 2
    blocks = half // (4 * CHUNK)
    shape = jax.ShapeDtypeStruct((blocks, BLOCK, LANES), jnp.float32)
    params = pltpu.CompilerParams(vmem_limit_bytes=8 * 1024 * 1024)
    cost = pl.CostEstimate(flops=0, bytes_accessed=8 * 1024 * 1024, transcendentals=0)
    rest_shape = jax.ShapeDtypeStruct((half, LANES), jnp.float32)
    keep, give, rest = pl.pallas_call(
        mix_first_kernel,
        out_shape=(shape, shape, rest_shape),
        in_specs=[IN_SMEM, IN_HBM, IN_VMEM, IN_VMEM],
        out_specs=(IN_VMEM, IN_VMEM, IN_VMEM),
        scratch_shapes=[
            pltpu.VMEM((half, LANES), jnp.float32),
            pltpu.SemaphoreType.DMA((PIECES + 1,)),
        ],
        compiler_params=params,
        cost_estimate=cost,
        name="mix_first",
    )(core, arrived, share, partner)
    second = pl.pallas_call(
        mix_second_kernel,
        out_shape=(shape, shape),
        in_specs=[IN_SMEM, IN_VMEM, IN_VMEM, IN_VMEM],
        out_specs=(IN_VMEM, IN_VMEM),
        compiler_params=params,
        cost_estimate=cost,
        name="mix_second",
    )(core, rest, share, partner)
    return (keep, give), second


def product(weights, value):
    high = value.astype(jnp.bfloat16)
    low = (value - high.astype(jnp.float32)).astype(jnp.bfloat16)
    return jnp.dot(
        weights,
        jnp.concatenate([high, low, high], axis=0),
        preferred_element_type=jnp.float32,
    )


def react_kernel(
    first, core_ref, mine_ref, other_ref, photo_ref, coupled_ref, precond_ref, production_ref, loss_ref, *rest
):
    out_ref, result_ref, sems = rest[-3:]
    blocks = mine_ref.shape[0]
    steps = result_ref.shape[0]
    each = blocks // steps
    width = each * LANES
    species = out_ref.shape[0]
    core = core_ref[0]
    copies = []
    for step in range(steps):
        columns = []
        for m in range(step * each, (step + 1) * each):
            mine, other = mine_ref[m], other_ref[m]
            columns.append(
                jnp.concatenate(
                    [jnp.where(core == 0, mine, other), jnp.where(core == 0, other, mine)], axis=0
                )
            )
        initial = jnp.concatenate(columns, axis=1)
        present = (initial[0:1] > 0.0).astype(jnp.float32)
        photo = jnp.concatenate(
            [photo_ref[first + m : first + m + 1, :] for m in range(step * each, (step + 1) * each)], axis=1
        )
        half_loss = jnp.concatenate([loss_ref[...]] * each, axis=1)
        source = jnp.concatenate([production_ref[...]] * each, axis=1) * photo
        current = initial
        for iteration in range(NEWTON):
            part_loss = half_loss * current
            moved = current - (initial + source) if iteration else -source
            misfit = moved - product(coupled_ref[...], current) + part_loss * current
            first_pass = product(precond_ref[...], misfit)
            second_pass = product(precond_ref[...], 2.0 * part_loss * first_pass)
            current = current - (first_pass - second_pass)
        result = current * present
        result_ref[step, :HALF] = result[:HALF]
        result_ref[step, HALF:] = result[BLOCK : BLOCK + species - HALF]
        start = first * LANES + step * width
        copy = pltpu.make_async_copy(
            result_ref.at[step], out_ref.at[:, start : start + width], sems.at[step]
        )
        copy.start()
        copies.append(copy)
    for copy in copies:
        copy.wait()


def react(part, species, core, mine, other, photo, weights, so_far):
    blocks = mine.shape[0]
    steps = 2
    width = blocks * LANES // steps
    in_specs = [IN_SMEM] + [IN_VMEM] * 7
    operands = [core, mine, other, photo, *weights]
    aliases = {}
    if so_far is not None:
        in_specs.append(pl.BlockSpec(memory_space=pl.ANY))
        operands.append(so_far)
        aliases = {len(operands) - 1: 0}

    def kernel(*refs):
        react_kernel(part * blocks, *refs)

    return pl.pallas_call(
        kernel,
        out_shape=jax.ShapeDtypeStruct((species, blocks * PARTS * LANES), jnp.float32),
        in_specs=in_specs,
        out_specs=pl.BlockSpec(memory_space=pl.ANY),
        scratch_shapes=[
            pltpu.VMEM((steps, species, width), jnp.float32),
            pltpu.SemaphoreType.DMA((steps,)),
        ],
        input_output_aliases=aliases,
        compiler_params=pltpu.CompilerParams(vmem_limit_bytes=16 * 1024 * 1024),
        cost_estimate=pl.CostEstimate(
            flops=6 * 2 * 256 * 512 * blocks * LANES, bytes_accessed=8 * 1024 * 1024, transcendentals=0
        ),
        name="react",
    )(*operands)


def spread(array, axis):
    gaps = [(0, 0)] * array.ndim
    first, second = jnp.split(array, [HALF], axis=axis)
    gaps[axis] = (0, BLOCK - first.shape[axis])
    first = jnp.pad(first, gaps)
    gaps[axis] = (0, BLOCK - second.shape[axis])
    return jnp.concatenate([first, jnp.pad(second, gaps)], axis=axis)


def split(matrix):
    padded = spread(spread(matrix, 0), 1)
    high = lax.reduce_precision(padded, 8, 7)
    low = padded - high
    return jnp.concatenate([high, high, low], axis=1).astype(jnp.bfloat16)


def column(vector):
    return jnp.broadcast_to(spread(vector, 0)[:, None], (ROWS, LANES))


SWAP = ((0, 1), (1, 0))


def shards(
    conc, dest_tile, mixing_share, partner, photolysis, production, loss, rates, pattern, precond
):
    species, parcels = conc.shape
    devices = lax.axis_size("lat") * lax.axis_size("chip") * 2
    rows = mixing_share.shape[0] // LANES
    core = lax.axis_index("core").astype(jnp.int32)[None]

    def both_tiles(array):
        array = array.reshape(rows, LANES)
        other = lax.ppermute(array, "core", SWAP)
        return jnp.where(core[0] == 0, jnp.stack([array, other]), jnp.stack([other, array]))

    share, index = both_tiles(mixing_share), both_tiles(partner)
    photo = photolysis.reshape(rows, LANES)
    coupled = rates * jnp.kron(pattern.astype(jnp.float32), jnp.ones((SB, SB), jnp.float32))
    weights = (
        split(time_step * coupled),
        split(precond),
        column(time_step * production),
        column(time_step * loss),
    )
    packed = pack(conc, dest_tile.reshape(parcels // LANES, LANES), devices)
    packed = packed.reshape(devices, CHUNK, 1, LANES)
    arrived = lax.all_to_all(
        packed, ("lat", "chip", "core"), split_axis=0, concat_axis=0, tiled=True
    ).reshape(devices * CHUNK, LANES)
    arrived, share, index, photo, *weights = lax.optimization_barrier(
        (arrived, share, index, photo, *weights)
    )
    halves = mix(core, arrived, share, index)
    others = [lax.ppermute(give, "core", SWAP) for _, give in halves]
    result = None
    for part in range(PARTS):
        result = react(part, species, core, halves[part][0], others[part], photo, weights, result)
    return result


def solution(mesh):
    lat_count, lon_count = mesh.devices.shape
    by_core = Mesh(mesh.devices.reshape(lat_count, lon_count // 2, 2), ("lat", "chip", "core"))
    tiles = ("lat", "chip", "core")
    placed = (P(None, tiles), P(tiles, None), P(tiles), P(tiles), P(tiles), P(), P(), P(), P(), P())
    return jax.shard_map(
        shards, mesh=by_core, in_specs=placed, out_specs=P(None, tiles), check_vma=False
    )
```

```python
import jax
import jax.numpy as jnp
from jax import lax
from jax.experimental import pallas as pl
from jax.experimental.pallas import tpu as pltpu
from jax.sharding import Mesh
from jax.sharding import PartitionSpec as P

SB = 15
NEWTON = 2
time_step = 0.5

LANES = 128
CAP = 32
QUARTER = 19
HALF = 4 * QUARTER
SENT = 2 * HALF
BLOCK = 80
ROWS = 2 * BLOCK
CHUNK = 3 * QUARTER
GROUP = 256
TOGETHER = 2
PIECES = 8


def regroup(parts):
    first, second, third, fourth = parts
    lane = lax.broadcasted_iota(jnp.int32, first.shape, 1)
    low_half = (lane & 64) == 0
    low_quarter = (lane & 32) == 0
    other_quarter = lane ^ 32

    def halves(a, b):
        moved = pltpu.roll(jnp.where(low_half, b, a), 64, 1)
        return jnp.where(low_half, a, moved), jnp.where(low_half, moved, b)

    def quarters(a, b):
        moved = jnp.take_along_axis(jnp.where(low_quarter, b, a), other_quarter, axis=1)
        return jnp.where(low_quarter, a, moved), jnp.where(low_quarter, moved, b)

    t0, t2 = halves(first, third)
    t1, t3 = halves(second, fourth)
    return (*quarters(t0, t1), *quarters(t2, t3))


def pack_kernel(conc_hbm, targets_hbm, out_hbm, out_ref, conc_ref, targets_ref, parts_ref, place_ref, group_ref, sums_ref, sems):
    species, parcels = conc_ref.shape
    read_conc = pltpu.make_async_copy(conc_hbm, conc_ref, sems.at[0])
    read_targets = pltpu.make_async_copy(targets_hbm, targets_ref, sems.at[1])
    read_targets.start()
    read_conc.start()
    read_targets.wait()
    row = lax.broadcasted_iota(jnp.int32, (LANES, LANES), 0)
    column = lax.broadcasted_iota(jnp.int32, (LANES, LANES), 1)
    earlier = (row < column).astype(jnp.float32).astype(jnp.bfloat16)
    sums_of = jnp.concatenate([earlier, jnp.ones((LANES, LANES), jnp.bfloat16)], axis=1)
    counted = jnp.zeros((LANES, LANES), jnp.float32)
    for block in range(parcels // LANES):
        span = slice(block * LANES, (block + 1) * LANES)
        targets = targets_ref[block : block + 1, :]
        onehot = (row == targets).astype(jnp.float32)
        sums = jnp.dot(onehot.astype(jnp.bfloat16), sums_of, preferred_element_type=jnp.float32)
        ranking = jnp.sum(onehot * (sums[:, :LANES] + counted), axis=0, keepdims=True)
        counted = counted + sums[:, LANES:]
        slot = targets * CAP + ranking.astype(jnp.int32)
        group_ref[:, span] = jnp.broadcast_to(slot // GROUP, (16, LANES))
        place = jnp.broadcast_to((slot % GROUP).astype(jnp.float32), (LANES, LANES))
        place = jnp.transpose(place).astype(jnp.int32)
        for side in range(GROUP // LANES):
            here = (place == column + side * LANES).astype(jnp.float32)
            place_ref[span, side * LANES : (side + 1) * LANES] = here.astype(jnp.bfloat16)
    read_conc.wait()
    conc = conc_ref[...]
    low = conc - conc.astype(jnp.bfloat16).astype(jnp.float32)
    filler = jnp.zeros((SENT - species, parcels), jnp.float32)
    parts_ref[...] = jnp.concatenate([conc, filler, low, filler], axis=0).astype(jnp.bfloat16)
    around = 16

    sent = around * 2 * CHUNK
    per_lat = around * 2 * CAP // GROUP

    def write(i):
        rows = slice(i * sent, (i + 1) * sent)
        return pltpu.make_async_copy(out_ref.at[rows], out_hbm.at[rows], sems.at[2 + i])

    def move(i):
        chosen = []
        for t in range(TOGETHER):
            mine = (group_ref[...] == i * TOGETHER + t).astype(jnp.float32).astype(jnp.bfloat16)
            chosen.append(parts_ref[...] * jnp.concatenate([mine] * (2 * SENT // 16), axis=0))
        return jnp.dot(
            jnp.concatenate(chosen, axis=0), place_ref[...], preferred_element_type=jnp.float32
        )

    def arrange(i, moved):
        for t in range(TOGETHER):
            base = 2 * t * SENT
            sums = moved[base : base + SENT] + moved[base + SENT : base + 2 * SENT]
            for side in range(GROUP // LANES):
                sums_ref[i % 2, t, side] = sums[:, side * LANES : (side + 1) * LANES]
        for t in range(TOGETHER):
            for side in range(GROUP // LANES):
                quad = (i * TOGETHER + t) * (GROUP // LANES) + side
                for half in range(2):
                    quarters = [
                        sums_ref[i % 2, t, side, half * HALF + QUARTER * j : half * HALF + QUARTER * (j + 1), :]
                        for j in range(4)
                    ]
                    for d, chunk in enumerate(regroup(quarters)):
                        chip = quad * 2 + d // 2
                        to = (chip * 2 + half) * CHUNK + (d % 2) * QUARTER
                        out_ref[to : to + QUARTER, :] = chunk
                        if d % 2 == 0:
                            west = chip // around * around + (chip + around - 1) % around
                            to = (west * 2 + half) * CHUNK + 2 * QUARTER
                            out_ref[to : to + QUARTER, :] = chunk
            if (i * TOGETHER + t + 1) % per_lat == 0:
                write((i * TOGETHER + t) // per_lat).start()

    steps = parcels * 2 // GROUP // TOGETHER
    for i in range(steps):
        arrange(i, move(i))
    for i in range(out_ref.shape[0] // sent):
        write(i).wait()


IN_VMEM = pl.BlockSpec(memory_space=pltpu.VMEM)
IN_HBM = pl.BlockSpec(memory_space=pltpu.HBM)
IN_SMEM = pl.BlockSpec(memory_space=pltpu.SMEM)


def pack(conc, targets, devices):
    parcels = conc.shape[1]
    return pl.pallas_call(
        pack_kernel,
        out_shape=jax.ShapeDtypeStruct((devices * CHUNK, LANES), jnp.float32),
        in_specs=[IN_HBM, IN_HBM],
        out_specs=IN_HBM,
        scratch_shapes=[
            pltpu.VMEM((devices * CHUNK, LANES), jnp.float32),
            pltpu.VMEM(conc.shape, jnp.float32),
            pltpu.VMEM(targets.shape, jnp.int32),
            pltpu.VMEM((2 * SENT, parcels), jnp.bfloat16),
            pltpu.VMEM((parcels, GROUP), jnp.bfloat16),
            pltpu.VMEM((16, parcels), jnp.int32),
            pltpu.VMEM((2, TOGETHER, GROUP // LANES, SENT, LANES), jnp.float32),
            pltpu.SemaphoreType.DMA((2 + 4,)),
        ],
        compiler_params=pltpu.CompilerParams(vmem_limit_bytes=63 * 1024 * 1024),
        name="pack",
    )(conc, targets)


def mix_block(m, place, core, arrived_ref, share_ref, partner_ref, keep_ref, give_ref):
    tiles = []
    for tile in range(3):
        parts = []
        for s in range(4):
            start = (m * 4 + s) * CHUNK + tile * QUARTER
            parts.append(arrived_ref[pl.ds(start, QUARTER), :])
        tiles.append(regroup(parts))
    mixed = []
    for tile in range(2):
        own, east = tiles[tile], tiles[tile + 1]
        index = jnp.broadcast_to(partner_ref[tile, pl.ds(place, 1), :], (QUARTER, LANES))
        chosen = [jnp.take_along_axis(e, index, axis=1) for e in east]
        present = (own[0][0:1] > 0.0).astype(jnp.float32)
        alive = (chosen[0][0:1] > 0.0).astype(jnp.float32)
        weight = share_ref[tile, pl.ds(place, 1), :] * present * alive
        weight = jnp.broadcast_to(weight, (QUARTER, LANES))
        mixed.append([o + weight * (c - o) for o, c in zip(own, chosen)])
    for j in range(4):
        rows = slice(QUARTER * j, QUARTER * (j + 1))
        keep_ref[m, rows, :] = jnp.where(core == 0, mixed[0][j], mixed[1][j])
        give_ref[m, rows, :] = jnp.where(core == 0, mixed[1][j], mixed[0][j])
    empty = jnp.zeros((BLOCK - HALF, LANES), jnp.float32)
    keep_ref[m, HALF:, :] = empty
    give_ref[m, HALF:, :] = empty


def mix_first_kernel(core_ref, arrived_hbm, share_ref, partner_ref, keep_ref, give_ref, rest_ref, land, sems):
    blocks = keep_ref.shape[0]
    each = blocks // PIECES
    length = each * 4 * CHUNK
    core = core_ref[0]
    reads = []
    for piece in range(PIECES):
        rows = slice(piece * length, (piece + 1) * length)
        reads.append(pltpu.make_async_copy(arrived_hbm.at[rows], land.at[rows], sems.at[piece]))
    rest = pltpu.make_async_copy(
        arrived_hbm.at[PIECES * length : 2 * PIECES * length], rest_ref, sems.at[PIECES]
    )
    for read in (*reads, rest):
        read.start()
    for piece in range(PIECES):
        reads[piece].wait()

        def body(m, carry):
            mix_block(m, m, core, land, share_ref, partner_ref, keep_ref, give_ref)
            return carry

        lax.fori_loop(piece * each, (piece + 1) * each, body, 0, unroll=2)
    rest.wait()


def mix_second_kernel(core_ref, rest_ref, share_ref, partner_ref, keep_ref, give_ref):
    blocks = keep_ref.shape[0]
    core = core_ref[0]

    def body(m, carry):
        mix_block(m, blocks + m, core, rest_ref, share_ref, partner_ref, keep_ref, give_ref)
        return carry

    lax.fori_loop(0, blocks, body, 0, unroll=2)


def mix(core, arrived, share, partner):
    half = arrived.shape[0] // 2
    blocks = half // (4 * CHUNK)
    shape = jax.ShapeDtypeStruct((blocks, BLOCK, LANES), jnp.float32)
    params = pltpu.CompilerParams(vmem_limit_bytes=8 * 1024 * 1024)
    cost = pl.CostEstimate(flops=0, bytes_accessed=8 * 1024 * 1024, transcendentals=0)
    rest_shape = jax.ShapeDtypeStruct((half, LANES), jnp.float32)
    keep, give, rest = pl.pallas_call(
        mix_first_kernel,
        out_shape=(shape, shape, rest_shape),
        in_specs=[IN_SMEM, IN_HBM, IN_VMEM, IN_VMEM],
        out_specs=(IN_VMEM, IN_VMEM, IN_VMEM),
        scratch_shapes=[
            pltpu.VMEM((half, LANES), jnp.float32),
            pltpu.SemaphoreType.DMA((PIECES + 1,)),
        ],
        compiler_params=params,
        cost_estimate=cost,
        name="mix_first",
    )(core, arrived, share, partner)
    second = pl.pallas_call(
        mix_second_kernel,
        out_shape=(shape, shape),
        in_specs=[IN_SMEM, IN_VMEM, IN_VMEM, IN_VMEM],
        out_specs=(IN_VMEM, IN_VMEM),
        compiler_params=params,
        cost_estimate=cost,
        name="mix_second",
    )(core, rest, share, partner)
    return (keep, give), second


def product(weights, value):
    high = value.astype(jnp.bfloat16)
    low = (value - high.astype(jnp.float32)).astype(jnp.bfloat16)
    return jnp.dot(
        weights,
        jnp.concatenate([high, low, high], axis=0),
        preferred_element_type=jnp.float32,
    )


def react_kernel(
    first, core_ref, mine_ref, other_ref, photo_ref, coupled_ref, precond_ref, production_ref, loss_ref, result_ref, done
):
    blocks = mine_ref.shape[0]
    steps, species, width = result_ref.shape
    each = blocks // steps
    core = core_ref[0]
    for step in range(steps):
        columns = []
        for m in range(step * each, (step + 1) * each):
            mine, other = mine_ref[m], other_ref[m]
            columns.append(
                jnp.concatenate(
                    [jnp.where(core == 0, mine, other), jnp.where(core == 0, other, mine)], axis=0
                )
            )
        initial = jnp.concatenate(columns, axis=1)
        present = (initial[0:1] > 0.0).astype(jnp.float32)
        photo = jnp.concatenate(
            [photo_ref[first + m : first + m + 1, :] for m in range(step * each, (step + 1) * each)], axis=1
        )
        half_loss = jnp.concatenate([loss_ref[...]] * each, axis=1)
        source = jnp.concatenate([production_ref[...]] * each, axis=1) * photo
        current = initial
        for iteration in range(NEWTON):
            part_loss = half_loss * current
            moved = current - (initial + source) if iteration else -source
            misfit = moved - product(coupled_ref[...], current) + part_loss * current
            first_pass = product(precond_ref[...], misfit)
            second_pass = product(precond_ref[...], 2.0 * part_loss * first_pass)
            current = current - (first_pass - second_pass)
        result = current * present
        result_ref[step, :HALF] = result[:HALF]
        result_ref[step, HALF:] = result[BLOCK : BLOCK + species - HALF]
        done(step)


def react_first_kernel(*refs):
    react_kernel(0, *refs, lambda step: None)


def react_second_kernel(*refs):
    *operands, earlier_ref, out_ref, result_ref, sems = refs
    steps, _, width = result_ref.shape
    blocks = steps * width // LANES
    copies = []

    def send(ref, step, place):
        columns = slice(place * width, (place + 1) * width)
        copy = pltpu.make_async_copy(ref.at[step], out_ref.at[:, columns], sems.at[place])
        copy.start()
        copies.append(copy)

    for step in range(steps):
        send(earlier_ref, step, step)
    react_kernel(blocks, *operands, result_ref, lambda step: send(result_ref, step, steps + step))
    for copy in copies:
        copy.wait()


def react(species, core, halves, others, photo, weights):
    blocks = others[0].shape[0]
    steps = 2
    shape = (steps, species, blocks * LANES // steps)
    params = pltpu.CompilerParams(vmem_limit_bytes=16 * 1024 * 1024)
    cost = pl.CostEstimate(
        flops=6 * 2 * 256 * 512 * blocks * LANES, bytes_accessed=8 * 1024 * 1024, transcendentals=0
    )
    earlier = pl.pallas_call(
        react_first_kernel,
        out_shape=jax.ShapeDtypeStruct(shape, jnp.float32),
        in_specs=[IN_SMEM] + [IN_VMEM] * 7,
        out_specs=IN_VMEM,
        compiler_params=params,
        cost_estimate=cost,
        name="react_first",
    )(core, halves[0][0], others[0], photo, *weights)
    return pl.pallas_call(
        react_second_kernel,
        out_shape=jax.ShapeDtypeStruct((species, 2 * blocks * LANES), jnp.float32),
        in_specs=[IN_SMEM] + [IN_VMEM] * 8,
        out_specs=pl.BlockSpec(memory_space=pl.ANY),
        scratch_shapes=[pltpu.VMEM(shape, jnp.float32), pltpu.SemaphoreType.DMA((2 * steps,))],
        compiler_params=params,
        cost_estimate=cost,
        name="react_second",
    )(core, halves[1][0], others[1], photo, *weights, earlier)


def spread(array, axis):
    gaps = [(0, 0)] * array.ndim
    first, second = jnp.split(array, [HALF], axis=axis)
    gaps[axis] = (0, BLOCK - first.shape[axis])
    first = jnp.pad(first, gaps)
    gaps[axis] = (0, BLOCK - second.shape[axis])
    return jnp.concatenate([first, jnp.pad(second, gaps)], axis=axis)


def split(matrix):
    padded = spread(spread(matrix, 0), 1)
    high = lax.reduce_precision(padded, 8, 7)
    low = padded - high
    return jnp.concatenate([high, high, low], axis=1).astype(jnp.bfloat16)


def column(vector):
    return jnp.broadcast_to(spread(vector, 0)[:, None], (ROWS, LANES))


SWAP = ((0, 1), (1, 0))


def shards(
    conc, dest_tile, mixing_share, partner, photolysis, production, loss, rates, pattern, precond
):
    species, parcels = conc.shape
    devices = lax.axis_size("lat") * lax.axis_size("chip") * 2
    rows = mixing_share.shape[0] // LANES
    core = lax.axis_index("core").astype(jnp.int32)[None]

    def both_tiles(array):
        array = array.reshape(rows, LANES)
        other = lax.ppermute(array, "core", SWAP)
        return jnp.where(core[0] == 0, jnp.stack([array, other]), jnp.stack([other, array]))

    share, index = both_tiles(mixing_share), both_tiles(partner)
    photo = photolysis.reshape(rows, LANES)
    coupled = rates * jnp.kron(pattern.astype(jnp.float32), jnp.ones((SB, SB), jnp.float32))
    weights = (
        split(time_step * coupled),
        split(precond),
        column(time_step * production),
        column(time_step * loss),
    )
    packed = pack(conc, dest_tile.reshape(parcels // LANES, LANES), devices)
    packed = packed.reshape(devices, CHUNK, 1, LANES)
    arrived = lax.all_to_all(
        packed, ("lat", "chip", "core"), split_axis=0, concat_axis=0, tiled=True
    ).reshape(devices * CHUNK, LANES)
    arrived, share, index, photo, *weights = lax.optimization_barrier(
        (arrived, share, index, photo, *weights)
    )
    halves = mix(core, arrived, share, index)
    others = [lax.ppermute(give, "core", SWAP) for _, give in halves]
    return react(species, core, halves, others, photo, weights)


def solution(mesh):
    lat_count, lon_count = mesh.devices.shape
    by_core = Mesh(mesh.devices.reshape(lat_count, lon_count // 2, 2), ("lat", "chip", "core"))
    tiles = ("lat", "chip", "core")
    placed = (P(None, tiles), P(tiles, None), P(tiles), P(tiles), P(tiles), P(), P(), P(), P(), P())
    return jax.shard_map(
        shards, mesh=by_core, in_specs=placed, out_specs=P(None, tiles), check_vma=False
    )
```

```python
import jax
import jax.numpy as jnp
from jax import lax
from jax.experimental import pallas as pl
from jax.experimental.pallas import tpu as pltpu
from jax.sharding import Mesh
from jax.sharding import PartitionSpec as P

SB = 15
NEWTON = 2
time_step = 0.5

LANES = 128
CAP = 32
SPARE = 8
QUARTER = 19
HALF = 4 * QUARTER
SENT = 2 * HALF
BLOCK = 80
ROWS = 2 * BLOCK
CHUNK = 3 * QUARTER
GROUP = 256
TOGETHER = 2
PIECES = 8


def regroup(parts):
    first, second, third, fourth = parts
    lane = lax.broadcasted_iota(jnp.int32, first.shape, 1)
    low_half = (lane & 64) == 0
    low_quarter = (lane & 32) == 0
    other_quarter = lane ^ 32

    def halves(a, b):
        moved = pltpu.roll(jnp.where(low_half, b, a), 64, 1)
        return jnp.where(low_half, a, moved), jnp.where(low_half, moved, b)

    def quarters(a, b):
        moved = jnp.take_along_axis(jnp.where(low_quarter, b, a), other_quarter, axis=1)
        return jnp.where(low_quarter, a, moved), jnp.where(low_quarter, moved, b)

    t0, t2 = halves(first, third)
    t1, t3 = halves(second, fourth)
    return (*quarters(t0, t1), *quarters(t2, t3))


def pack_kernel(conc_hbm, targets_hbm, out_hbm, out_ref, conc_ref, targets_ref, parts_ref, place_ref, group_ref, sums_ref, sems):
    species, parcels = conc_ref.shape
    read_conc = pltpu.make_async_copy(conc_hbm, conc_ref, sems.at[0])
    read_targets = pltpu.make_async_copy(targets_hbm, targets_ref, sems.at[1])
    read_targets.start()
    read_conc.start()
    read_targets.wait()
    row = lax.broadcasted_iota(jnp.int32, (LANES, LANES), 0)
    column = lax.broadcasted_iota(jnp.int32, (LANES, LANES), 1)
    earlier = (row < column).astype(jnp.float32).astype(jnp.bfloat16)
    sums_of = jnp.concatenate([earlier, jnp.ones((LANES, LANES), jnp.bfloat16)], axis=1)
    counted = jnp.zeros((LANES, LANES), jnp.float32)
    for block in range(parcels // LANES):
        span = slice(block * LANES, (block + 1) * LANES)
        targets = targets_ref[block : block + 1, :]
        onehot = (row == targets).astype(jnp.float32)
        sums = jnp.dot(onehot.astype(jnp.bfloat16), sums_of, preferred_element_type=jnp.float32)
        ranking = jnp.sum(onehot * (sums[:, :LANES] + counted), axis=0, keepdims=True)
        counted = counted + sums[:, LANES:]
        slot = targets * CAP + ranking.astype(jnp.int32)
        group_ref[:, span] = jnp.broadcast_to(slot // GROUP, (16, LANES))
        place = jnp.broadcast_to((slot % GROUP).astype(jnp.float32), (LANES, LANES))
        place = jnp.transpose(place).astype(jnp.int32)
        for side in range(GROUP // LANES):
            here = (place == column + side * LANES).astype(jnp.float32)
            place_ref[span, side * LANES : (side + 1) * LANES] = here.astype(jnp.bfloat16)
    read_conc.wait()
    conc = conc_ref[...]
    low = conc - conc.astype(jnp.bfloat16).astype(jnp.float32)
    filler = jnp.zeros((SENT - species, parcels), jnp.float32)
    parts_ref[...] = jnp.concatenate([conc, filler, low, filler], axis=0).astype(jnp.bfloat16)
    around = 16

    sent = around * 2 * CHUNK
    per_lat = around * 2 * CAP // GROUP

    def write(i):
        rows = slice(i * sent, (i + 1) * sent)
        return pltpu.make_async_copy(out_ref.at[rows], out_hbm.at[rows], sems.at[2 + i])

    def move(i):
        chosen = []
        for t in range(TOGETHER):
            mine = (group_ref[...] == i * TOGETHER + t).astype(jnp.float32).astype(jnp.bfloat16)
            chosen.append(parts_ref[...] * jnp.concatenate([mine] * (2 * SENT // 16), axis=0))
        return jnp.dot(
            jnp.concatenate(chosen, axis=0), place_ref[...], preferred_element_type=jnp.float32
        )

    def arrange(i, moved):
        for t in range(TOGETHER):
            base = 2 * t * SENT
            sums = moved[base : base + SENT] + moved[base + SENT : base + 2 * SENT]
            for side in range(GROUP // LANES):
                sums_ref[i % 2, t, side] = sums[:, side * LANES : (side + 1) * LANES]
        for t in range(TOGETHER):
            for side in range(GROUP // LANES):
                quad = (i * TOGETHER + t) * (GROUP // LANES) + side
                for half in range(2):
                    quarters = [
                        sums_ref[i % 2, t, side, half * HALF + QUARTER * j : half * HALF + QUARTER * (j + 1), :]
                        for j in range(4)
                    ]
                    for d, chunk in enumerate(regroup(quarters)):
                        chip = quad * 2 + d // 2
                        to = (chip * 2 + half) * CHUNK + (d % 2) * QUARTER
                        out_ref[to : to + QUARTER, :] = chunk
                        if d % 2 == 0:
                            west = chip // around * around + (chip + around - 1) % around
                            to = (west * 2 + half) * CHUNK + 2 * QUARTER
                            out_ref[to : to + QUARTER, :] = chunk
            if (i * TOGETHER + t + 1) % per_lat == 0:
                write((i * TOGETHER + t) // per_lat).start()

    steps = parcels * 2 // GROUP // TOGETHER
    for i in range(steps):
        arrange(i, move(i))
    for i in range(out_hbm.shape[0] // sent):
        write(i).wait()


IN_VMEM = pl.BlockSpec(memory_space=pltpu.VMEM)
IN_HBM = pl.BlockSpec(memory_space=pltpu.HBM)
IN_SMEM = pl.BlockSpec(memory_space=pltpu.SMEM)


def pack(conc, targets, devices):
    parcels = conc.shape[1]
    return pl.pallas_call(
        pack_kernel,
        out_shape=jax.ShapeDtypeStruct((devices * CHUNK, LANES), jnp.float32),
        in_specs=[IN_HBM, IN_HBM],
        out_specs=IN_HBM,
        scratch_shapes=[
            pltpu.VMEM((devices * CHUNK + SPARE, LANES), jnp.float32),
            pltpu.VMEM(conc.shape, jnp.float32),
            pltpu.VMEM(targets.shape, jnp.int32),
            pltpu.VMEM((2 * SENT, parcels), jnp.bfloat16),
            pltpu.VMEM((parcels, GROUP), jnp.bfloat16),
            pltpu.VMEM((16, parcels), jnp.int32),
            pltpu.VMEM((2, TOGETHER, GROUP // LANES, SENT, LANES), jnp.float32),
            pltpu.SemaphoreType.DMA((2 + 4,)),
        ],
        compiler_params=pltpu.CompilerParams(vmem_limit_bytes=63 * 1024 * 1024),
        name="pack",
    )(conc, targets)


def mix_block(m, place, core, arrived_ref, share_ref, partner_ref, keep_ref, give_ref):
    tiles = []
    for tile in range(3):
        parts = []
        for s in range(4):
            start = (m * 4 + s) * CHUNK + tile * QUARTER
            parts.append(arrived_ref[pl.ds(start, QUARTER), :])
        tiles.append(regroup(parts))
    mixed = []
    for tile in range(2):
        own, east = tiles[tile], tiles[tile + 1]
        index = jnp.broadcast_to(partner_ref[tile, pl.ds(place, 1), :], (QUARTER, LANES))
        chosen = [jnp.take_along_axis(e, index, axis=1) for e in east]
        present = (own[0][0:1] > 0.0).astype(jnp.float32)
        alive = (chosen[0][0:1] > 0.0).astype(jnp.float32)
        weight = share_ref[tile, pl.ds(place, 1), :] * present * alive
        weight = jnp.broadcast_to(weight, (QUARTER, LANES))
        mixed.append([o + weight * (c - o) for o, c in zip(own, chosen)])
    for j in range(4):
        rows = slice(QUARTER * j, QUARTER * (j + 1))
        keep_ref[m, rows, :] = jnp.where(core == 0, mixed[0][j], mixed[1][j])
        give_ref[m, rows, :] = jnp.where(core == 0, mixed[1][j], mixed[0][j])
    empty = jnp.zeros((BLOCK - HALF, LANES), jnp.float32)
    keep_ref[m, HALF:, :] = empty
    give_ref[m, HALF:, :] = empty


def mix_first_kernel(core_ref, arrived_hbm, share_ref, partner_ref, keep_ref, give_ref, rest_ref, land, sems):
    blocks = keep_ref.shape[0]
    each = blocks // PIECES
    length = each * 4 * CHUNK
    core = core_ref[0]
    reads = []
    for piece in range(PIECES):
        rows = slice(piece * length, (piece + 1) * length)
        reads.append(pltpu.make_async_copy(arrived_hbm.at[rows], land.at[rows], sems.at[piece]))
    rest = pltpu.make_async_copy(
        arrived_hbm.at[PIECES * length : 2 * PIECES * length],
        rest_ref.at[0 : PIECES * length],
        sems.at[PIECES],
    )
    for read in (*reads, rest):
        read.start()
    for piece in range(PIECES):
        reads[piece].wait()

        def body(m, carry):
            mix_block(m, m, core, land, share_ref, partner_ref, keep_ref, give_ref)
            return carry

        lax.fori_loop(piece * each, (piece + 1) * each, body, 0, unroll=2)
    rest.wait()


def mix_second_kernel(core_ref, rest_ref, share_ref, partner_ref, keep_ref, give_ref):
    blocks = keep_ref.shape[0]
    core = core_ref[0]

    def body(m, carry):
        mix_block(m, blocks + m, core, rest_ref, share_ref, partner_ref, keep_ref, give_ref)
        return carry

    lax.fori_loop(0, blocks, body, 0, unroll=2)


def mix(core, arrived, share, partner):
    half = arrived.shape[0] // 2
    blocks = half // (4 * CHUNK)
    shape = jax.ShapeDtypeStruct((blocks, BLOCK, LANES), jnp.float32)
    params = pltpu.CompilerParams(vmem_limit_bytes=8 * 1024 * 1024)
    cost = pl.CostEstimate(flops=0, bytes_accessed=8 * 1024 * 1024, transcendentals=0)
    rest_shape = jax.ShapeDtypeStruct((half + SPARE, LANES), jnp.float32)
    keep, give, rest = pl.pallas_call(
        mix_first_kernel,
        out_shape=(shape, shape, rest_shape),
        in_specs=[IN_SMEM, IN_HBM, IN_VMEM, IN_VMEM],
        out_specs=(IN_VMEM, IN_VMEM, IN_VMEM),
        scratch_shapes=[
            pltpu.VMEM((half + SPARE, LANES), jnp.float32),
            pltpu.SemaphoreType.DMA((PIECES + 1,)),
        ],
        compiler_params=params,
        cost_estimate=cost,
        name="mix_first",
    )(core, arrived, share, partner)
    second = pl.pallas_call(
        mix_second_kernel,
        out_shape=(shape, shape),
        in_specs=[IN_SMEM, IN_VMEM, IN_VMEM, IN_VMEM],
        out_specs=(IN_VMEM, IN_VMEM),
        compiler_params=params,
        cost_estimate=cost,
        name="mix_second",
    )(core, rest, share, partner)
    return (keep, give), second


def product(weights, value):
    high = value.astype(jnp.bfloat16)
    low = (value - high.astype(jnp.float32)).astype(jnp.bfloat16)
    return jnp.dot(
        weights,
        jnp.concatenate([high, low, high], axis=0),
        preferred_element_type=jnp.float32,
    )


def react_kernel(
    first, core_ref, mine_ref, other_ref, photo_ref, coupled_ref, precond_ref, production_ref, loss_ref, result_ref, done
):
    blocks = mine_ref.shape[0]
    steps, species, width = result_ref.shape
    each = blocks // steps
    core = core_ref[0]
    for step in range(steps):
        columns = []
        for m in range(step * each, (step + 1) * each):
            mine, other = mine_ref[m], other_ref[m]
            columns.append(
                jnp.concatenate(
                    [jnp.where(core == 0, mine, other), jnp.where(core == 0, other, mine)], axis=0
                )
            )
        initial = jnp.concatenate(columns, axis=1)
        present = (initial[0:1] > 0.0).astype(jnp.float32)
        photo = jnp.concatenate(
            [photo_ref[first + m : first + m + 1, :] for m in range(step * each, (step + 1) * each)], axis=1
        )
        half_loss = jnp.concatenate([loss_ref[...]] * each, axis=1)
        source = jnp.concatenate([production_ref[...]] * each, axis=1) * photo
        current = initial
        for iteration in range(NEWTON):
            part_loss = half_loss * current
            moved = current - (initial + source) if iteration else -source
            misfit = moved - product(coupled_ref[...], current) + part_loss * current
            first_pass = product(precond_ref[...], misfit)
            second_pass = product(precond_ref[...], 2.0 * part_loss * first_pass)
            current = current - (first_pass - second_pass)
        result = current * present
        result_ref[step, :HALF] = result[:HALF]
        result_ref[step, HALF:] = result[BLOCK : BLOCK + species - HALF]
        done(step)


def react_first_kernel(*refs):
    react_kernel(0, *refs, lambda step: None)


def react_second_kernel(*refs):
    *operands, earlier_ref, out_ref, result_ref, sems = refs
    steps, _, width = result_ref.shape
    blocks = steps * width // LANES
    copies = []

    def send(ref, step, place):
        columns = slice(place * width, (place + 1) * width)
        copy = pltpu.make_async_copy(ref.at[step], out_ref.at[:, columns], sems.at[place])
        copy.start()
        copies.append(copy)

    for step in range(steps):
        send(earlier_ref, step, step)
    react_kernel(blocks, *operands, result_ref, lambda step: send(result_ref, step, steps + step))
    for copy in copies:
        copy.wait()


def react(species, core, halves, others, photo, weights):
    blocks = others[0].shape[0]
    steps = 2
    shape = (steps, species, blocks * LANES // steps)
    params = pltpu.CompilerParams(vmem_limit_bytes=16 * 1024 * 1024)
    cost = pl.CostEstimate(
        flops=6 * 2 * 256 * 512 * blocks * LANES, bytes_accessed=8 * 1024 * 1024, transcendentals=0
    )
    earlier = pl.pallas_call(
        react_first_kernel,
        out_shape=jax.ShapeDtypeStruct(shape, jnp.float32),
        in_specs=[IN_SMEM] + [IN_VMEM] * 7,
        out_specs=IN_VMEM,
        compiler_params=params,
        cost_estimate=cost,
        name="react_first",
    )(core, halves[0][0], others[0], photo, *weights)
    return pl.pallas_call(
        react_second_kernel,
        out_shape=jax.ShapeDtypeStruct((species, 2 * blocks * LANES), jnp.float32),
        in_specs=[IN_SMEM] + [IN_VMEM] * 8,
        out_specs=pl.BlockSpec(memory_space=pl.ANY),
        scratch_shapes=[pltpu.VMEM(shape, jnp.float32), pltpu.SemaphoreType.DMA((2 * steps,))],
        compiler_params=params,
        cost_estimate=cost,
        name="react_second",
    )(core, halves[1][0], others[1], photo, *weights, earlier)


def spread(array, axis):
    gaps = [(0, 0)] * array.ndim
    first, second = jnp.split(array, [HALF], axis=axis)
    gaps[axis] = (0, BLOCK - first.shape[axis])
    first = jnp.pad(first, gaps)
    gaps[axis] = (0, BLOCK - second.shape[axis])
    return jnp.concatenate([first, jnp.pad(second, gaps)], axis=axis)


def split(matrix):
    padded = spread(spread(matrix, 0), 1)
    high = lax.reduce_precision(padded, 8, 7)
    low = padded - high
    return jnp.concatenate([high, high, low], axis=1).astype(jnp.bfloat16)


def column(vector):
    return jnp.broadcast_to(spread(vector, 0)[:, None], (ROWS, LANES))


SWAP = ((0, 1), (1, 0))


def shards(
    conc, dest_tile, mixing_share, partner, photolysis, production, loss, rates, pattern, precond
):
    species, parcels = conc.shape
    devices = lax.axis_size("lat") * lax.axis_size("chip") * 2
    rows = mixing_share.shape[0] // LANES
    core = lax.axis_index("core").astype(jnp.int32)[None]

    def both_tiles(array):
        array = array.reshape(rows, LANES)
        other = lax.ppermute(array, "core", SWAP)
        return jnp.where(core[0] == 0, jnp.stack([array, other]), jnp.stack([other, array]))

    share, index = both_tiles(mixing_share), both_tiles(partner)
    photo = photolysis.reshape(rows, LANES)
    coupled = rates * jnp.kron(pattern.astype(jnp.float32), jnp.ones((SB, SB), jnp.float32))
    weights = (
        split(time_step * coupled),
        split(precond),
        column(time_step * production),
        column(time_step * loss),
    )
    packed = pack(conc, dest_tile.reshape(parcels // LANES, LANES), devices)
    packed = packed.reshape(devices, CHUNK, 1, LANES)
    arrived = lax.all_to_all(
        packed, ("lat", "chip", "core"), split_axis=0, concat_axis=0, tiled=True
    ).reshape(devices * CHUNK, LANES)
    arrived, share, index, photo, *weights = lax.optimization_barrier(
        (arrived, share, index, photo, *weights)
    )
    halves = mix(core, arrived, share, index)
    others = [lax.ppermute(give, "core", SWAP) for _, give in halves]
    return react(species, core, halves, others, photo, weights)


def solution(mesh):
    lat_count, lon_count = mesh.devices.shape
    by_core = Mesh(mesh.devices.reshape(lat_count, lon_count // 2, 2), ("lat", "chip", "core"))
    tiles = ("lat", "chip", "core")
    placed = (P(None, tiles), P(tiles, None), P(tiles), P(tiles), P(tiles), P(), P(), P(), P(), P())
    return jax.shard_map(
        shards, mesh=by_core, in_specs=placed, out_specs=P(None, tiles), check_vma=False
    )
```

```python
import jax
import jax.numpy as jnp
from jax import lax
from jax.experimental import pallas as pl
from jax.experimental.pallas import tpu as pltpu
from jax.sharding import Mesh
from jax.sharding import PartitionSpec as P

SB = 15
NEWTON = 2
time_step = 0.5

LANES = 128
CAP = 32
SPARE = 8
QUARTER = 19
HALF = 4 * QUARTER
SENT = 2 * HALF
BLOCK = 80
ROWS = 2 * BLOCK
CHUNK = 3 * QUARTER
GROUP = 256
TOGETHER = 2
PIECES = 8


def regroup(parts):
    first, second, third, fourth = parts
    lane = lax.broadcasted_iota(jnp.int32, first.shape, 1)
    low_half = (lane & 64) == 0
    low_quarter = (lane & 32) == 0
    other_quarter = lane ^ 32

    def halves(a, b):
        moved = pltpu.roll(jnp.where(low_half, b, a), 64, 1)
        return jnp.where(low_half, a, moved), jnp.where(low_half, moved, b)

    def quarters(a, b):
        moved = jnp.take_along_axis(jnp.where(low_quarter, b, a), other_quarter, axis=1)
        return jnp.where(low_quarter, a, moved), jnp.where(low_quarter, moved, b)

    t0, t2 = halves(first, third)
    t1, t3 = halves(second, fourth)
    return (*quarters(t0, t1), *quarters(t2, t3))


def pack_kernel(conc_hbm, targets_hbm, out_hbm, out_ref, conc_ref, targets_ref, parts_ref, place_ref, group_ref, sums_ref, sems):
    species, parcels = conc_ref.shape
    read_conc = pltpu.make_async_copy(conc_hbm, conc_ref, sems.at[0])
    read_targets = pltpu.make_async_copy(targets_hbm, targets_ref, sems.at[1])
    read_targets.start()
    read_conc.start()
    read_targets.wait()
    row = lax.broadcasted_iota(jnp.int32, (LANES, LANES), 0)
    column = lax.broadcasted_iota(jnp.int32, (LANES, LANES), 1)
    earlier = (row < column).astype(jnp.float32).astype(jnp.bfloat16)
    sums_of = jnp.concatenate([earlier, jnp.ones((LANES, LANES), jnp.bfloat16)], axis=1)
    counted = jnp.zeros((LANES, LANES), jnp.float32)
    for block in range(parcels // LANES):
        span = slice(block * LANES, (block + 1) * LANES)
        targets = targets_ref[block : block + 1, :]
        onehot = (row == targets).astype(jnp.float32)
        sums = jnp.dot(onehot.astype(jnp.bfloat16), sums_of, preferred_element_type=jnp.float32)
        ranking = jnp.sum(onehot * (sums[:, :LANES] + counted), axis=0, keepdims=True)
        counted = counted + sums[:, LANES:]
        slot = targets * CAP + ranking.astype(jnp.int32)
        group_ref[:, span] = jnp.broadcast_to(slot // GROUP, (16, LANES))
        place = jnp.broadcast_to((slot % GROUP).astype(jnp.float32), (LANES, LANES))
        place = jnp.transpose(place).astype(jnp.int32)
        for side in range(GROUP // LANES):
            here = (place == column + side * LANES).astype(jnp.float32)
            place_ref[span, side * LANES : (side + 1) * LANES] = here.astype(jnp.bfloat16)
    read_conc.wait()
    conc = conc_ref[...]
    low = conc - conc.astype(jnp.bfloat16).astype(jnp.float32)
    filler = jnp.zeros((SENT - species, parcels), jnp.float32)
    parts_ref[...] = jnp.concatenate([conc, filler, low, filler], axis=0).astype(jnp.bfloat16)
    around = 16

    sent = around * 2 * CHUNK
    per_lat = around * 2 * CAP // GROUP

    def write(i):
        rows = slice(i * sent, (i + 1) * sent)
        return pltpu.make_async_copy(out_ref.at[rows], out_hbm.at[rows], sems.at[2 + i])

    def move(i):
        chosen = []
        for t in range(TOGETHER):
            mine = (group_ref[...] == i * TOGETHER + t).astype(jnp.float32).astype(jnp.bfloat16)
            chosen.append(parts_ref[...] * jnp.concatenate([mine] * (2 * SENT // 16), axis=0))
        return jnp.dot(
            jnp.concatenate(chosen, axis=0), place_ref[...], preferred_element_type=jnp.float32
        )

    def arrange(i, moved):
        for t in range(TOGETHER):
            base = 2 * t * SENT
            sums = moved[base : base + SENT] + moved[base + SENT : base + 2 * SENT]
            for side in range(GROUP // LANES):
                sums_ref[i % 2, t, side] = sums[:, side * LANES : (side + 1) * LANES]
        for t in range(TOGETHER):
            for side in range(GROUP // LANES):
                quad = (i * TOGETHER + t) * (GROUP // LANES) + side
                for half in range(2):
                    quarters = [
                        sums_ref[i % 2, t, side, half * HALF + QUARTER * j : half * HALF + QUARTER * (j + 1), :]
                        for j in range(4)
                    ]
                    for d, chunk in enumerate(regroup(quarters)):
                        chip = quad * 2 + d // 2
                        to = (chip * 2 + half) * CHUNK + (d % 2) * QUARTER
                        out_ref[to : to + QUARTER, :] = chunk
                        if d % 2 == 0:
                            west = chip // around * around + (chip + around - 1) % around
                            to = (west * 2 + half) * CHUNK + 2 * QUARTER
                            out_ref[to : to + QUARTER, :] = chunk
            if (i * TOGETHER + t + 1) % per_lat == 0:
                write((i * TOGETHER + t) // per_lat).start()

    steps = parcels * 2 // GROUP // TOGETHER
    for i in range(steps):
        arrange(i, move(i))
    for i in range(out_hbm.shape[0] // sent):
        write(i).wait()


IN_VMEM = pl.BlockSpec(memory_space=pltpu.VMEM)
IN_HBM = pl.BlockSpec(memory_space=pltpu.HBM)
IN_SMEM = pl.BlockSpec(memory_space=pltpu.SMEM)


def pack(conc, targets, devices):
    parcels = conc.shape[1]
    return pl.pallas_call(
        pack_kernel,
        out_shape=jax.ShapeDtypeStruct((devices * CHUNK, LANES), jnp.float32),
        in_specs=[IN_HBM, IN_HBM],
        out_specs=IN_HBM,
        scratch_shapes=[
            pltpu.VMEM((devices * CHUNK + SPARE, LANES), jnp.float32),
            pltpu.VMEM(conc.shape, jnp.float32),
            pltpu.VMEM(targets.shape, jnp.int32),
            pltpu.VMEM((2 * SENT, parcels), jnp.bfloat16),
            pltpu.VMEM((parcels, GROUP), jnp.bfloat16),
            pltpu.VMEM((16, parcels), jnp.int32),
            pltpu.VMEM((2, TOGETHER, GROUP // LANES, SENT, LANES), jnp.float32),
            pltpu.SemaphoreType.DMA((2 + 4,)),
        ],
        compiler_params=pltpu.CompilerParams(vmem_limit_bytes=63 * 1024 * 1024),
        name="pack",
    )(conc, targets)


def mix_block(m, place, core, arrived_ref, share_ref, partner_ref, keep_ref, give_ref):
    tiles = []
    for tile in range(3):
        parts = []
        for s in range(4):
            start = (m * 4 + s) * CHUNK + tile * QUARTER
            parts.append(arrived_ref[pl.ds(start, QUARTER), :])
        tiles.append(regroup(parts))
    mixed = []
    for tile in range(2):
        own, east = tiles[tile], tiles[tile + 1]
        index = jnp.broadcast_to(partner_ref[tile, pl.ds(place, 1), :], (QUARTER, LANES))
        chosen = [jnp.take_along_axis(e, index, axis=1) for e in east]
        present = (own[0][0:1] > 0.0).astype(jnp.float32)
        alive = (chosen[0][0:1] > 0.0).astype(jnp.float32)
        weight = share_ref[tile, pl.ds(place, 1), :] * present * alive
        weight = jnp.broadcast_to(weight, (QUARTER, LANES))
        mixed.append([o + weight * (c - o) for o, c in zip(own, chosen)])
    for j in range(4):
        rows = slice(QUARTER * j, QUARTER * (j + 1))
        keep_ref[m, rows, :] = jnp.where(core == 0, mixed[0][j], mixed[1][j])
        give_ref[m, rows, :] = jnp.where(core == 0, mixed[1][j], mixed[0][j])
    empty = jnp.zeros((BLOCK - HALF, LANES), jnp.float32)
    keep_ref[m, HALF:, :] = empty
    give_ref[m, HALF:, :] = empty


def mix_first_kernel(core_ref, arrived_hbm, share_ref, partner_ref, keep_ref, give_ref, rest_ref, land, sems):
    blocks = keep_ref.shape[0]
    each = blocks // PIECES
    length = each * 4 * CHUNK
    core = core_ref[0]
    reads = []
    for piece in range(PIECES):
        rows = slice(piece * length, (piece + 1) * length)
        reads.append(pltpu.make_async_copy(arrived_hbm.at[rows], land.at[rows], sems.at[piece]))
    rest = pltpu.make_async_copy(
        arrived_hbm.at[PIECES * length : 2 * PIECES * length],
        rest_ref.at[0 : PIECES * length],
        sems.at[PIECES],
    )
    for read in (*reads, rest):
        read.start()
    for piece in range(PIECES):
        reads[piece].wait()

        def body(m, carry):
            mix_block(m, m, core, land, share_ref, partner_ref, keep_ref, give_ref)
            return carry

        lax.fori_loop(piece * each, (piece + 1) * each, body, 0, unroll=2)
    rest.wait()


def mix_second_kernel(core_ref, rest_ref, share_ref, partner_ref, keep_ref, give_ref):
    blocks = keep_ref.shape[0]
    core = core_ref[0]

    def body(m, carry):
        mix_block(m, blocks + m, core, rest_ref, share_ref, partner_ref, keep_ref, give_ref)
        return carry

    lax.fori_loop(0, blocks, body, 0, unroll=2)


def mix(core, arrived, share, partner):
    half = arrived.shape[0] // 2
    blocks = half // (4 * CHUNK)
    shape = jax.ShapeDtypeStruct((blocks, BLOCK, LANES), jnp.float32)
    params = pltpu.CompilerParams(vmem_limit_bytes=8 * 1024 * 1024)
    cost = pl.CostEstimate(flops=0, bytes_accessed=8 * 1024 * 1024, transcendentals=0)
    rest_shape = jax.ShapeDtypeStruct((half + SPARE, LANES), jnp.float32)
    keep, give, rest = pl.pallas_call(
        mix_first_kernel,
        out_shape=(shape, shape, rest_shape),
        in_specs=[IN_SMEM, IN_HBM, IN_VMEM, IN_VMEM],
        out_specs=(IN_VMEM, IN_VMEM, IN_VMEM),
        scratch_shapes=[
            pltpu.VMEM((half + SPARE, LANES), jnp.float32),
            pltpu.SemaphoreType.DMA((PIECES + 1,)),
        ],
        compiler_params=params,
        cost_estimate=cost,
        name="mix_first",
    )(core, arrived, share, partner)
    second = pl.pallas_call(
        mix_second_kernel,
        out_shape=(shape, shape),
        in_specs=[IN_SMEM, IN_VMEM, IN_VMEM, IN_VMEM],
        out_specs=(IN_VMEM, IN_VMEM),
        compiler_params=params,
        cost_estimate=cost,
        name="mix_second",
    )(core, rest, share, partner)
    return (keep, give), second


def parts_of(value):
    high = value.astype(jnp.bfloat16)
    low = (value - high.astype(jnp.float32)).astype(jnp.bfloat16)
    return jnp.concatenate([high, low, high], axis=0)


def product(weights, parts):
    return jnp.dot(weights, parts, preferred_element_type=jnp.float32)


def react_kernel(
    first, core_ref, mine_ref, other_ref, photo_ref, coupled_ref, precond_ref, production_ref, loss_ref, result_ref, done
):
    blocks = mine_ref.shape[0]
    steps, species, width = result_ref.shape
    each = blocks // steps
    core = core_ref[0]

    def newton(step):
        columns = []
        for m in range(step * each, (step + 1) * each):
            mine, other = mine_ref[m], other_ref[m]
            columns.append(
                jnp.concatenate(
                    [jnp.where(core == 0, mine, other), jnp.where(core == 0, other, mine)], axis=0
                )
            )
        initial = jnp.concatenate(columns, axis=1)
        present = (initial[0:1] > 0.0).astype(jnp.float32)
        photo = jnp.concatenate(
            [photo_ref[first + m : first + m + 1, :] for m in range(step * each, (step + 1) * each)], axis=1
        )
        half_loss = jnp.concatenate([loss_ref[...]] * each, axis=1)
        source = jnp.concatenate([production_ref[...]] * each, axis=1) * photo
        current = initial
        parts = parts_of(current)
        for iteration in range(NEWTON):
            yield
            linear = product(coupled_ref[...], parts)
            yield
            part_loss = half_loss * current
            moved = current - (initial + source) if iteration else -source
            parts = parts_of(moved - linear + part_loss * current)
            yield
            first_pass = product(precond_ref[...], parts)
            yield
            parts = parts_of(2.0 * part_loss * first_pass)
            yield
            second_pass = product(precond_ref[...], parts)
            yield
            current = current - (first_pass - second_pass)
            if iteration < NEWTON - 1:
                parts = parts_of(current)
        result = current * present
        result_ref[step, :HALF] = result[:HALF]
        result_ref[step, HALF:] = result[BLOCK : BLOCK + species - HALF]
        done(step)

    running = [newton(step) for step in range(steps)]
    while running:
        for work in list(running):
            if next(work, "done") == "done":
                running.remove(work)


def react_first_kernel(*refs):
    react_kernel(0, *refs, lambda step: None)


def react_second_kernel(*refs):
    *operands, earlier_ref, out_ref, result_ref, sems = refs
    steps, _, width = result_ref.shape
    blocks = steps * width // LANES
    copies = []

    def send(ref, step, place):
        columns = slice(place * width, (place + 1) * width)
        copy = pltpu.make_async_copy(ref.at[step], out_ref.at[:, columns], sems.at[place])
        copy.start()
        copies.append(copy)

    for step in range(steps):
        send(earlier_ref, step, step)
    react_kernel(blocks, *operands, result_ref, lambda step: send(result_ref, step, steps + step))
    for copy in copies:
        copy.wait()


def react(species, core, halves, others, photo, weights):
    blocks = others[0].shape[0]
    steps = 4
    shape = (steps, species, blocks * LANES // steps)
    params = pltpu.CompilerParams(vmem_limit_bytes=16 * 1024 * 1024)
    cost = pl.CostEstimate(
        flops=6 * 2 * 256 * 512 * blocks * LANES, bytes_accessed=8 * 1024 * 1024, transcendentals=0
    )
    earlier = pl.pallas_call(
        react_first_kernel,
        out_shape=jax.ShapeDtypeStruct(shape, jnp.float32),
        in_specs=[IN_SMEM] + [IN_VMEM] * 7,
        out_specs=IN_VMEM,
        compiler_params=params,
        cost_estimate=cost,
        name="react_first",
    )(core, halves[0][0], others[0], photo, *weights)
    return pl.pallas_call(
        react_second_kernel,
        out_shape=jax.ShapeDtypeStruct((species, 2 * blocks * LANES), jnp.float32),
        in_specs=[IN_SMEM] + [IN_VMEM] * 8,
        out_specs=pl.BlockSpec(memory_space=pl.ANY),
        scratch_shapes=[pltpu.VMEM(shape, jnp.float32), pltpu.SemaphoreType.DMA((2 * steps,))],
        compiler_params=params,
        cost_estimate=cost,
        name="react_second",
    )(core, halves[1][0], others[1], photo, *weights, earlier)


def spread(array, axis):
    gaps = [(0, 0)] * array.ndim
    first, second = jnp.split(array, [HALF], axis=axis)
    gaps[axis] = (0, BLOCK - first.shape[axis])
    first = jnp.pad(first, gaps)
    gaps[axis] = (0, BLOCK - second.shape[axis])
    return jnp.concatenate([first, jnp.pad(second, gaps)], axis=axis)


def split(matrix):
    padded = spread(spread(matrix, 0), 1)
    high = lax.reduce_precision(padded, 8, 7)
    low = padded - high
    return jnp.concatenate([high, high, low], axis=1).astype(jnp.bfloat16)


def column(vector):
    return jnp.broadcast_to(spread(vector, 0)[:, None], (ROWS, LANES))


SWAP = ((0, 1), (1, 0))


def shards(
    conc, dest_tile, mixing_share, partner, photolysis, production, loss, rates, pattern, precond
):
    species, parcels = conc.shape
    devices = lax.axis_size("lat") * lax.axis_size("chip") * 2
    rows = mixing_share.shape[0] // LANES
    core = lax.axis_index("core").astype(jnp.int32)[None]

    def both_tiles(array):
        array = array.reshape(rows, LANES)
        other = lax.ppermute(array, "core", SWAP)
        return jnp.where(core[0] == 0, jnp.stack([array, other]), jnp.stack([other, array]))

    share, index = both_tiles(mixing_share), both_tiles(partner)
    photo = photolysis.reshape(rows, LANES)
    coupled = rates * jnp.kron(pattern.astype(jnp.float32), jnp.ones((SB, SB), jnp.float32))
    weights = (
        split(time_step * coupled),
        split(precond),
        column(time_step * production),
        column(time_step * loss),
    )
    packed = pack(conc, dest_tile.reshape(parcels // LANES, LANES), devices)
    packed = packed.reshape(devices, CHUNK, 1, LANES)
    arrived = lax.all_to_all(
        packed, ("lat", "chip", "core"), split_axis=0, concat_axis=0, tiled=True
    ).reshape(devices * CHUNK, LANES)
    arrived, share, index, photo, *weights = lax.optimization_barrier(
        (arrived, share, index, photo, *weights)
    )
    halves = mix(core, arrived, share, index)
    others = [lax.ppermute(give, "core", SWAP) for _, give in halves]
    return react(species, core, halves, others, photo, weights)


def solution(mesh):
    lat_count, lon_count = mesh.devices.shape
    by_core = Mesh(mesh.devices.reshape(lat_count, lon_count // 2, 2), ("lat", "chip", "core"))
    tiles = ("lat", "chip", "core")
    placed = (P(None, tiles), P(tiles, None), P(tiles), P(tiles), P(tiles), P(), P(), P(), P(), P())
    return jax.shard_map(
        shards, mesh=by_core, in_specs=placed, out_specs=P(None, tiles), check_vma=False
    )
```
